32 devices in a mesh: ctx: 16 (over z, y, x), ch: 2 (over core).
Axes of the slice: x: 2, y: 2, z: 4, core: 2. Of those that a mesh axis runs over, the one named last changes fastest.
Arguments:
- grad_out: bfloat16 [12288, 4096], P('ctx', 'ch'), may hold values from -6 to 6
- block_input: bfloat16 [12288, 4096], P('ctx', 'ch'), may hold values from -40 to 40
- norm_gain: bfloat16 [4096], P('ch'), may hold values from 0.5 to 1.5
- queries: bfloat16 [12288, 4096], P('ctx', 'ch'), may hold values from -6 to 6
- keys: bfloat16 [12288, 4096], P('ctx', 'ch'), may hold values from -6 to 6
- values: bfloat16 [12288, 4096], P('ctx', 'ch'), may hold values from -6 to 6
- filters: bfloat16 [256, 128], P('ch'), may hold values from -0.5 to 0.5
- doc_starts: int32 [16, 4], P('ctx'), may hold values from 0 to 767, as said below
- in_weight: bfloat16 [4096, 3, 4096], P('ctx', None, 'ch'), may hold values from -0.09375 to 0.09375
- out_weight: bfloat16 [4096, 4096], P('ch', 'ctx'), may hold values from -0.09375 to 0.09375
Outputs:
- grad_input: bfloat16 [12288, 4096], P('ctx', 'ch')
The draws below stay inside these ranges and needn't reach their ends.
Inputs may be any that keep to these rules, and one draw needn't show every extreme that they name: `doc_starts`: each row holds 4 distinct document starts of one slab as offsets within the slab, in ascending order; the first slab's first start is 0.
All inputs are finite; a program needn't handle non-finite values.
Results may differ from the reference program's by a relative error of at most 0.013.
Values may be sent and summed in bfloat16 or wider, within the bound.
No kernel may reach another device: no remote copies, remote signals or barrier semaphores. Data moves between devices by JAX's collectives and lax.ppermute only.
A program may use at most 192 MiB of HBM per device.

```python
import math
import jax
import jax.numpy as jnp
from jax import lax

D = 4096
FILTER_LEN = 128
GROUP_WIDTH = 16
DOCS = 4
TOK_DEV = 768
TOKENS = 12288
SLABS = 16
GROUPS = 256
CHAN_WIDTH = 2048
N_CH = 2


def draw_block_input(key, part):
    first_key, second_key, third_key = jax.random.split(key, 3)
    row_scale = jnp.exp(jax.random.uniform(first_key, (TOKENS, 1), jnp.float32, math.log(0.3), math.log(3.0)))
    feature_pos = jnp.arange(D, dtype=jnp.float32) / D
    rising = math.log(3.0)
    base = jnp.clip(jax.random.normal(third_key, (TOKENS, D), jnp.float32), -3.5, 3.5)
    jitter = jax.random.uniform(second_key, (D,), jnp.float32, -0.5, 0.5)
    col_scale = jnp.exp(rising * (feature_pos - 0.5) + jitter)[None, :]
    return (base * row_scale * col_scale).astype(jnp.bfloat16)


def draw_doc_starts(key, part):
    slab_keys = jax.random.split(key, SLABS)

    def one_slab(slab_key):
        chosen = jax.random.permutation(slab_key, TOK_DEV - 1)[:DOCS] + 1
        return jnp.sort(chosen)
    starts = jax.vmap(one_slab)(slab_keys).astype(jnp.int32)
    starts = starts.at[0, 0].set(0)
    starts = starts.at[SLABS - 1, DOCS - 1].set(TOK_DEV - 1)
    return starts


def level_of(key, dims, cuts, least, high):
    level, own = 1.0, jax.random.fold_in(key, 6)
    for axis_at, shards_of in cuts:
        steps = jnp.exp(jax.random.uniform(jax.random.fold_in(own, axis_at), (shards_of,), jnp.float32, least / len(cuts), high / len(cuts)))
        level = level * jnp.repeat(steps, dims[axis_at] // shards_of).reshape([-1 if axis == axis_at else 1 for axis in range(len(dims))])
    return level


def noise(key, dims, width, limit, cuts=(), held_as=jnp.bfloat16):
    gain = level_of(key, dims, cuts, -0.22, 0.18) if cuts else 1.0
    entries = jax.random.normal(key, dims, jnp.float32) * width * gain
    return jnp.minimum(jnp.maximum(entries, -limit), limit).astype(held_as)


def setup_inputs(seed: int = 0) -> dict:
    arg_keys = jax.random.split(jax.random.key(seed), 11)
    return {
        "grad_out": noise(arg_keys[0], (TOKENS, D), 1.0, 6.0, ((0, 16), (1, 2))),
        "block_input": draw_block_input(jax.random.fold_in(arg_keys[10], 71), 0),
        "norm_gain": jnp.clip(1.0 + 0.1 * jax.random.normal(arg_keys[2], (D,), jnp.float32), 0.5, 1.5).astype(jnp.bfloat16),
        "queries": noise(arg_keys[3], (TOKENS, D), 1.0, 6.0, ((0, 16), (1, 2))),
        "keys": noise(arg_keys[4], (TOKENS, D), 1.0, 6.0, ((0, 16), (1, 2))),
        "values": noise(arg_keys[5], (TOKENS, D), 1.0, 6.0, ((0, 16), (1, 2))),
        "filters": noise(arg_keys[6], (GROUPS, FILTER_LEN), FILTER_LEN ** -0.5, 0.5, ((0, 2),)),
        "doc_starts": draw_doc_starts(jax.random.fold_in(arg_keys[10], 71), 0),
        "in_weight": noise(arg_keys[8], (D, 3, D), D ** -0.5, 0.09375, ((0, 16), (2, 2))),
        "out_weight": noise(arg_keys[9], (D, D), D ** -0.5, 0.09375, ((0, 2), (1, 16))),
    }


epsilon = 1e-05

def toeplitz_table(filters):
    tap_index = jnp.arange(FILTER_LEN, dtype=jnp.int32)[:, None] + FILTER_LEN - jnp.arange(2 * FILTER_LEN, dtype=jnp.int32)[None, :]
    valid = (tap_index >= 0) & (tap_index < FILTER_LEN)
    picked = jnp.take(filters.astype(jnp.float32), jnp.clip(tap_index, 0, FILTER_LEN - 1), axis=1)
    return jnp.where(valid[None], picked, jnp.float32(0.0))

def reference(grad_out, block_input, norm_gain, queries, keys, values, filters, doc_starts, in_weight, out_weight):
    slab_base = jnp.arange(SLABS, dtype=jnp.int32) * TOK_DEV
    starts = (doc_starts + slab_base[:, None]).reshape(-1).astype(jnp.int32)
    position = jnp.arange(TOKENS, dtype=jnp.int32)
    last_start = lax.optimization_barrier(jnp.max(jnp.where(starts[None, :] <= position[:, None], starts[None, :], -1), axis=1)).astype(jnp.int32)
    tile_count = TOKENS // FILTER_LEN
    table = toeplitz_table(filters)
    flipped = table[:, ::-1, ::-1]
    products = (keys.astype(jnp.float32) * values.astype(jnp.float32)).astype(jnp.bfloat16)
    padded_prod = jnp.concatenate([jnp.zeros((FILTER_LEN, D), jnp.bfloat16), products], axis=0)

    def forward_tile(tile_idx):
        source = lax.dynamic_slice_in_dim(padded_prod, tile_idx * FILTER_LEN, 2 * FILTER_LEN, 0)
        source = source.astype(jnp.float32).reshape(2 * FILTER_LEN, GROUPS, GROUP_WIDTH)
        row_last = lax.dynamic_slice_in_dim(last_start, tile_idx * FILTER_LEN, FILTER_LEN, 0)
        col_pos = (tile_idx - 1) * FILTER_LEN + jnp.arange(2 * FILTER_LEN, dtype=jnp.int32)
        allowed = col_pos[None, :] >= row_last[:, None]
        masked = jnp.where(allowed[None], table, jnp.float32(0.0))
        return jnp.einsum('gtp,pgc->tgc', masked, source).reshape(FILTER_LEN, D)
    mixed = lax.map(forward_tile, jnp.arange(tile_count, dtype=jnp.int32)).reshape(TOKENS, D)
    mix_grad = jnp.dot(grad_out, out_weight.T, preferred_element_type=jnp.float32)
    q_grad = (mix_grad * mixed).astype(jnp.bfloat16)
    w_grad = (mix_grad * queries.astype(jnp.float32)).astype(jnp.bfloat16)
    padded_grad = jnp.concatenate([w_grad, jnp.zeros((FILTER_LEN, D), jnp.bfloat16)], axis=0)
    padded_last = jnp.concatenate([last_start, jnp.full((FILTER_LEN,), TOKENS, jnp.int32)], axis=0)

    def backward_tile(tile_idx):
        source = lax.dynamic_slice_in_dim(padded_grad, tile_idx * FILTER_LEN, 2 * FILTER_LEN, 0)
        source = source.astype(jnp.float32).reshape(2 * FILTER_LEN, GROUPS, GROUP_WIDTH)
        col_last = lax.dynamic_slice_in_dim(padded_last, tile_idx * FILTER_LEN, 2 * FILTER_LEN, 0)
        row_pos = tile_idx * FILTER_LEN + jnp.arange(FILTER_LEN, dtype=jnp.int32)
        allowed = row_pos[:, None] >= col_last[None, :]
        masked = jnp.where(allowed[None], flipped, jnp.float32(0.0))
        return jnp.einsum('gst,tgc->sgc', masked, source).reshape(FILTER_LEN, D)
    conv_grad = lax.map(backward_tile, jnp.arange(tile_count, dtype=jnp.int32)).reshape(TOKENS, D)
    k_grad = (conv_grad * values.astype(jnp.float32)).astype(jnp.bfloat16)
    v_grad = (conv_grad * keys.astype(jnp.float32)).astype(jnp.bfloat16)
    stacked = jnp.stack([q_grad, k_grad, v_grad], axis=1)

    def group_step(running, group_idx):
        columns = lax.dynamic_slice_in_dim(stacked, group_idx * CHAN_WIDTH, CHAN_WIDTH, 2).reshape(TOKENS, 3 * CHAN_WIDTH)
        weight_part = lax.dynamic_slice_in_dim(in_weight, group_idx * CHAN_WIDTH, CHAN_WIDTH, 2).reshape(D, 3 * CHAN_WIDTH)
        partial_value = jnp.dot(columns, weight_part.T, preferred_element_type=jnp.float32).astype(jnp.bfloat16)
        partial_value = lax.optimization_barrier(partial_value)
        return (running + partial_value.astype(jnp.float32), None)
    norm_grad, unused = lax.scan(group_step, jnp.zeros((TOKENS, D), jnp.float32), jnp.arange(N_CH, dtype=jnp.int32))
    source_in = block_input.astype(jnp.float32)
    scaled = norm_gain.astype(jnp.float32)[None, :] * norm_grad
    square_sum = lax.optimization_barrier(jnp.sum(source_in * source_in, axis=1, keepdims=True))
    cross_sum = lax.optimization_barrier(jnp.sum(scaled * source_in, axis=1, keepdims=True))
    inverse = lax.rsqrt(square_sum / D + epsilon)
    result = grad_out.astype(jnp.float32) + inverse * scaled - source_in * (inverse * inverse * inverse) * cross_sum / D
    return result.astype(jnp.bfloat16)
```

```python
import functools

import jax
import jax.numpy as jnp
from jax import lax
from jax.experimental import pallas as pl
from jax.experimental.pallas import tpu as pltpu
from jax.sharding import Mesh
from jax.sharding import PartitionSpec as P

LANES = 128
EPSILON = 1e-05
VMEM_BYTES = 48 * 1024 * 1024

SWAP = [(0, 0), (1, 2), (2, 1), (3, 3)]
CYCLE = [(0, 2), (1, 0), (2, 3), (3, 1)]
PAIR = [(0, 1), (1, 0)]


def swapped(block):
    return lax.ppermute(block, ("x", "c"), SWAP)


def after(block, *others):
    others = [o for o in others if o is not None]
    if not others:
        return block
    return lax.optimization_barrier((block, *others))[0]


def params(parallel):
    return pltpu.CompilerParams(
        dimension_semantics=("arbitrary",) * parallel, vmem_limit_bytes=VMEM_BYTES
    )


def toeplitz_into(table_ref, base_ref, taps, count):
    for q in range(count):
        row = jnp.broadcast_to(base_ref[q : q + 1, :], (taps, 2 * taps))
        band = pltpu.roll(row, 0, 1, stride=1, stride_axis=0)
        table_ref[q * taps : (q + 1) * taps, :] = band.astype(table_ref.dtype)


def banded(table_ref, keep, source, taps, count):
    table = table_ref[...].reshape(count, taps, 2 * taps)
    masked = (table * keep.astype(jnp.bfloat16)[None]).reshape(count * taps, 2 * taps)
    wide = jnp.dot(masked, source, preferred_element_type=jnp.float32)
    width = source.shape[1]
    owner = lax.broadcasted_iota(jnp.int32, (taps, width), 1) // (width // count)
    total = wide[:taps]
    for q in range(1, count):
        total = jnp.where(owner == q, wide[q * taps : (q + 1) * taps], total)
    return total


def forward_kernel(
    taps, count, base_ref, last_ref, tail_ref, keys_ref, values_ref, mix_ref, out_ref, table_ref, prev_ref
):
    tile = pl.program_id(1)

    @pl.when(tile == 0)
    def _():
        toeplitz_into(table_ref, base_ref, taps, count)
        prev_ref[...] = tail_ref[...]

    current = (keys_ref[...].astype(jnp.float32) * values_ref[...].astype(jnp.float32)).astype(
        jnp.bfloat16
    )
    source = jnp.concatenate([prev_ref[...], current], axis=0)
    col = lax.broadcasted_iota(jnp.int32, (taps, 2 * taps), 1) + (tile - 1) * taps
    keep = jnp.where(col >= last_ref[...], 1.0, 0.0)
    mixed = banded(table_ref, keep, source, taps, count)
    out_ref[...] = (mix_ref[...] * mixed).astype(out_ref.dtype)
    prev_ref[...] = current


def backward_kernel(
    taps, count, tiles, base_ref, last_ref, next_last_ref, head_ref, keys_ref, values_ref, grad_ref,
    k_ref, v_ref, table_ref, next_ref,
):
    tile = tiles - 1 - pl.program_id(1)

    @pl.when(tile == tiles - 1)
    def _():
        toeplitz_into(table_ref, base_ref, taps, count)
        next_ref[...] = head_ref[...]

    current = grad_ref[...]
    source = jnp.concatenate([current, next_ref[...]], axis=0)
    row = lax.broadcasted_iota(jnp.int32, (taps, 2 * taps), 0) + tile * taps
    last = jnp.concatenate([last_ref[...], next_last_ref[...]], axis=1)
    keep = jnp.where(row >= last, 1.0, 0.0)
    conv = banded(table_ref, keep, source, taps, count)
    k_ref[...] = (conv * values_ref[...].astype(jnp.float32)).astype(k_ref.dtype)
    v_ref[...] = (conv * keys_ref[...].astype(jnp.float32)).astype(v_ref.dtype)
    next_ref[...] = current


def forward_conv(base, last, tail, keys, values, mix, taps, per):
    rows, width = keys.shape
    tile = pl.BlockSpec((taps, LANES), lambda g, i: (i, g))
    return pl.pallas_call(
        functools.partial(forward_kernel, taps, per),
        grid=(width // LANES, rows // taps),
        in_specs=[
            pl.BlockSpec((per, 2 * taps), lambda g, i: (g, 0)),
            pl.BlockSpec((taps, 1), lambda g, i: (i, 0)),
            pl.BlockSpec((taps, LANES), lambda g, i: (0, g)),
            tile, tile, tile,
        ],
        out_specs=tile,
        out_shape=jax.ShapeDtypeStruct((rows, width), jnp.bfloat16),
        scratch_shapes=[
            pltpu.VMEM((per * taps, 2 * taps), jnp.bfloat16),
            pltpu.VMEM((taps, LANES), jnp.bfloat16),
        ],
        compiler_params=params(2),
        cost_estimate=pl.CostEstimate(
            flops=2 * rows * width * 2 * taps * per, bytes_accessed=rows * width * 10, transcendentals=0
        ),
        name="forward_conv",
    )(base, last, tail, keys, values, mix)


def backward_conv(base, last, head, keys, values, grad, taps, per):
    rows, width = keys.shape
    tiles = rows // taps
    tile = pl.BlockSpec((taps, LANES), lambda g, i: (tiles - 1 - i, g))
    out = jax.ShapeDtypeStruct((rows, width), jnp.bfloat16)
    return pl.pallas_call(
        functools.partial(backward_kernel, taps, per, tiles),
        grid=(width // LANES, tiles),
        in_specs=[
            pl.BlockSpec((per, 2 * taps), lambda g, i: (g, 0)),
            pl.BlockSpec((1, taps), lambda g, i: (0, tiles - 1 - i)),
            pl.BlockSpec((1, taps), lambda g, i: (0, tiles - i)),
            pl.BlockSpec((taps, LANES), lambda g, i: (0, g)),
            tile, tile, tile,
        ],
        out_specs=[tile, tile],
        out_shape=[out, out],
        scratch_shapes=[
            pltpu.VMEM((per * taps, 2 * taps), jnp.bfloat16),
            pltpu.VMEM((taps, LANES), jnp.bfloat16),
        ],
        compiler_params=params(2),
        cost_estimate=pl.CostEstimate(
            flops=2 * rows * width * 2 * taps * per, bytes_accessed=rows * width * 10, transcendentals=0
        ),
        name="backward_conv",
    )(base, last, last, head, keys, values, grad)


NT = (((1,), (1,)), ((), ()))


def mix_kernel(at_ref, left_ref, right_ref, own_ref, sib_ref, out_ref):
    step = pl.program_id(1)
    both = lax.dot_general(left_ref[...], own_ref[0], NT, preferred_element_type=jnp.float32)
    both += lax.dot_general(right_ref[...], sib_ref[0], NT, preferred_element_type=jnp.float32)

    @pl.when(step == 0)
    def _():
        out_ref[...] = both

    @pl.when(step > 0)
    def _():
        out_ref[...] += both


def mix_matmul(at, grads, own, sib):
    rows = grads.shape[0]
    blocks, width, feats = own.shape
    cols = min(width, 1024)
    return pl.pallas_call(
        mix_kernel,
        grid_spec=pltpu.PrefetchScalarGridSpec(
            num_scalar_prefetch=1,
            grid=(width // cols, blocks),
            in_specs=[
                pl.BlockSpec((rows, feats), lambda n, j, at: (0, at[0, j])),
                pl.BlockSpec((rows, feats), lambda n, j, at: (0, at[1, j])),
                pl.BlockSpec((1, cols, feats), lambda n, j, at: (j, n, 0)),
                pl.BlockSpec((1, cols, feats), lambda n, j, at: (j, n, 0)),
            ],
            out_specs=pl.BlockSpec((rows, cols), lambda n, j, at: (0, n)),
        ),
        out_shape=jax.ShapeDtypeStruct((rows, width), jnp.float32),
        compiler_params=params(2),
        cost_estimate=pl.CostEstimate(
            flops=4 * rows * blocks * width * feats,
            bytes_accessed=4 * blocks * width * feats + 4 * rows * width,
            transcendentals=0,
        ),
        name="mix_matmul",
    )(at, grads, grads, own, sib)


def project_kernel(branches, blocks, *refs):
    grads, weights, out_ref = refs[:branches], refs[branches:-1], refs[-1]
    for n in range(blocks):
        total = None
        for b in range(branches):
            part = lax.dot_general(
                grads[b][...], weights[n * branches + b][...], NT, preferred_element_type=jnp.float32
            )
            total = part if total is None else total + part
        out_ref[n] = total.astype(out_ref.dtype)


def project(grads, weights):
    branches, blocks = len(grads), len(weights)
    rows, width = grads[0].shape
    feats = weights[0][0].shape[0]
    step = rows // 2
    return pl.pallas_call(
        functools.partial(project_kernel, branches, blocks),
        grid=(rows // step,),
        in_specs=[pl.BlockSpec((step, width), lambda i: (i, 0))] * branches
        + [pl.BlockSpec((feats, width), lambda i: (0, 0))] * (branches * blocks),
        out_specs=pl.BlockSpec((blocks, step, feats), lambda i: (0, i, 0)),
        out_shape=jax.ShapeDtypeStruct((blocks, rows, feats), jnp.bfloat16),
        compiler_params=params(1),
        cost_estimate=pl.CostEstimate(
            flops=2 * rows * width * branches * feats * blocks,
            bytes_accessed=2 * branches * width * (rows + feats * blocks),
            transcendentals=0,
        ),
        name="project",
    )(*grads, *[w for block in weights for w in block])


def pick_kernel(at_ref, own_ref, sib_ref, input_ref, gain_ref, norm_ref, cross_ref):
    step = pl.program_id(0)
    ours = (lax.broadcasted_iota(jnp.int32, own_ref.shape[1:], 0) * 0 + at_ref[2, step]) == 1
    norm = jnp.where(ours, own_ref[0].astype(jnp.float32), sib_ref[0].astype(jnp.float32))
    norm_ref[...] = norm.astype(norm_ref.dtype)
    part = jnp.sum(
        gain_ref[...].astype(jnp.float32) * norm * input_ref[...].astype(jnp.float32),
        axis=1,
        keepdims=True,
    )

    @pl.when(step == 0)
    def _():
        cross_ref[...] = part

    @pl.when(step > 0)
    def _():
        cross_ref[...] += part


def pick(at, own, sib, block_input, gain):
    rows, width = block_input.shape
    feats = own.shape[2]
    return pl.pallas_call(
        pick_kernel,
        grid_spec=pltpu.PrefetchScalarGridSpec(
            num_scalar_prefetch=1,
            grid=(width // feats,),
            in_specs=[
                pl.BlockSpec((1, rows, feats), lambda j, at: (at[0, j], 0, 0)),
                pl.BlockSpec((1, rows, feats), lambda j, at: (at[1, j], 0, 0)),
                pl.BlockSpec((rows, feats), lambda j, at: (0, j)),
                pl.BlockSpec((1, feats), lambda j, at: (0, j)),
            ],
            out_specs=[
                pl.BlockSpec((rows, feats), lambda j, at: (0, j)),
                pl.BlockSpec((rows, 1), lambda j, at: (0, 0)),
            ],
        ),
        out_shape=[
            jax.ShapeDtypeStruct((rows, width), jnp.bfloat16),
            jax.ShapeDtypeStruct((rows, 1), jnp.float32),
        ],
        compiler_params=params(1),
        name="pick",
    )(at, own, sib, block_input, gain)


def on_device(
    ring,
    n_chan,
    grad_out,
    block_input,
    norm_gain,
    queries,
    keys,
    values,
    filters,
    doc_starts,
    in_weight,
    out_weight,
):
    rows, width = grad_out.shape
    groups, taps = filters.shape
    feats, branches = in_weight.shape[:2]
    count = len(ring)
    per = LANES * groups // width
    features = feats * 2 * count
    o, x, h, c = (lax.axis_index(a) for a in ("o", "x", "h", "c"))
    order = jnp.array(ring, jnp.int32)
    place = jnp.array([ring.index(i) for i in range(count)], jnp.int32)
    position = place[o]

    source_in = block_input.astype(jnp.float32)
    square_sum = lax.psum(jnp.sum(source_in * source_in, axis=1), ("h", "c"))

    out_w = swapped(out_weight)
    starts = swapped(doc_starts)[0]
    taps_own = swapped(filters)
    grad_half = swapped(after(grad_out, out_w))
    grad_other = lax.ppermute(after(grad_out, out_w), ("x", "c"), CYCLE)
    in_w = [swapped(after(in_weight[:, b], grad_half, grad_other)) for b in range(branches)]
    own_q = swapped(after(queries, *in_w))
    own_k = swapped(after(keys, own_q))
    own_v = swapped(after(values, own_k))

    forth = [(ring[i], ring[(i + 1) % count]) for i in range(count)]
    back = [(b, a) for a, b in forth]
    chains = [out_w] + in_w
    hops = [
        (count // 2, (count - 1) // 2) if n % 2 == 0 else ((count - 1) // 2, count // 2)
        for n in range(1 + branches)
    ]
    held = {(n, 0): chains[n] for n in range(1 + branches)}
    for way, route, sign in ((0, forth, -1), (1, back, 1)):
        items = [(0, s) for s in range(1, hops[0][way] + 1)]
        items += [
            (n, s)
            for s in range(1, count // 2 + 1)
            for n in range(1, 1 + branches)
            if s <= hops[n][way]
        ]
        done = [None, None]
        for n, s in items:
            block = after(held[n, sign * (s - 1)], done[-2])
            held[n, sign * s] = lax.ppermute(block, ("o",), route)
            done.append(held[n, sign * s])
    far = count // 2

    def block_of(n, distance):
        if abs(distance) == far:
            return held[n, -far] if (n, -far) in held else held[n, far]
        return held[n, distance]

    distances = [0]
    for s in range(1, far):
        distances += [-s, s]
    distances += [far]
    sources = order[(position + jnp.array(distances, jnp.int32)) % count]

    own_out = jnp.stack([block_of(0, d) for d in distances])
    sib_out = lax.ppermute(own_out, "c", PAIR)
    if n_chan > 1:
        grad_half = lax.all_gather(grad_half, "h", axis=1, tiled=True)
        grad_other = lax.all_gather(grad_other, "h", axis=1, tiled=True)
    grads = jnp.concatenate([grad_half, grad_other], axis=1)
    wide = width // feats

    def column(parity):
        block = sources * 2 + parity
        owner = block // wide
        side = jnp.where(owner % 2 == x, 0, 1)
        return side * (n_chan * wide) + (owner // 2) * wide + block % wide

    mix_grad = mix_matmul(jnp.stack([column(c), column(1 - c)]), grads, own_out, sib_out)

    slabs = 2 * count
    onward = [(i, i + 1) for i in range(slabs - 1)]
    backward = [(i + 1, i) for i in range(slabs - 1)]
    positions = jnp.arange(rows, dtype=jnp.int32)
    prior = lax.ppermute(starts[-1:], ("o", "c"), onward)
    last_start = jnp.maximum(
        jnp.max(
            jnp.where(starts[None, :] <= positions[:, None], starts[None, :], -rows), axis=1
        ),
        prior[0] - rows,
    )
    head_last = lax.ppermute(last_start[:taps], ("o", "c"), backward)
    taps32 = taps_own.astype(jnp.float32)
    edge = jnp.zeros((groups, taps), jnp.float32)
    base_back = jnp.concatenate([taps32, edge], axis=1)
    base_fore = jnp.concatenate([edge[:, :1], taps32[:, ::-1], edge[:, 1:]], axis=1)

    w_grad = (mix_grad * own_q.astype(jnp.float32)).astype(jnp.bfloat16)
    head = lax.ppermute(w_grad[:taps], ("o", "c"), backward)
    padded_last = jnp.concatenate([last_start, head_last + rows])[None]
    k_grad, v_grad = backward_conv(
        base_back, padded_last, head, own_k, own_v, w_grad, taps, per
    )
    tail = (
        own_k[rows - taps :].astype(jnp.float32) * own_v[rows - taps :].astype(jnp.float32)
    ).astype(jnp.bfloat16)
    tail = lax.ppermute(tail, ("o", "c"), onward)
    q_grad = forward_conv(
        base_fore, last_start[:, None], tail, own_k, own_v, mix_grad, taps, per
    )

    own_grads = [q_grad, k_grad, v_grad]
    sib_grads = [lax.ppermute(g, "c", PAIR) for g in own_grads]
    batches = [distances[:3]] + [distances[i : i + 2] for i in range(3, len(distances), 2)]
    norms = []
    for batch in batches:
        weights = [[block_of(1 + b, d) for b in range(branches)] for d in batch]
        ours = project(own_grads, weights)
        theirs = project(sib_grads, weights)
        keep = jnp.where(c == x, ours, theirs)
        send = jnp.where(c == x, theirs, ours)
        received = lax.ppermute(send, "x", PAIR)
        norms.append((keep.astype(jnp.float32) + received.astype(jnp.float32)).astype(jnp.bfloat16))
    if n_chan > 1:
        norm = jnp.concatenate(norms, axis=0)
        slot = jnp.zeros((count,), jnp.int32).at[sources].set(jnp.arange(count, dtype=jnp.int32))
        norm = lax.psum_scatter(
            jnp.take(norm, slot, axis=0), "h", scatter_dimension=0, tiled=True
        )
        other = lax.ppermute(norm, "c", PAIR)
        slot = jnp.arange(count, dtype=jnp.int32) - h * (count // n_chan)
    else:
        norm = jnp.concatenate(norms, axis=0)
        other = jnp.concatenate([lax.ppermute(n, "c", PAIR) for n in norms], axis=0)
        slot = jnp.zeros((count,), jnp.int32).at[sources].set(jnp.arange(count, dtype=jnp.int32))
    mine = (h * 2 + c) * wide + jnp.arange(wide, dtype=jnp.int32)
    slots = slot[mine // 2]
    at = jnp.stack([slots, slots, (mine % 2 == c).astype(jnp.int32)])
    norm_grad, cross = pick(at, norm, other, block_input, norm_gain[None])
    cross_sum = lax.psum(cross, ("h", "c"))
    inverse = lax.rsqrt(square_sum / features + EPSILON)[:, None]
    scaled = norm_gain.astype(jnp.float32)[None, :] * norm_grad.astype(jnp.float32)
    result = (
        grad_out.astype(jnp.float32)
        + inverse * scaled
        - source_in * (inverse * inverse * inverse) * cross_sum / features
    )
    return result.astype(jnp.bfloat16)


def solution(mesh):
    outer, n_chan = mesh.shape["ctx"] // 2, mesh.shape["ch"] // 2
    split = Mesh(mesh.devices.reshape(outer, 2, n_chan, 2), ("o", "x", "h", "c"))
    ring = list(range(0, outer, 2)) + list(range(outer - 1, 0, -2))
    tok, chan = ("o", "x"), ("h", "c")
    placed = (
        P(tok, chan),
        P(tok, chan),
        P(chan),
        P(tok, chan),
        P(tok, chan),
        P(tok, chan),
        P(chan, None),
        P(tok, None),
        P(tok, None, chan),
        P(chan, tok),
    )
    return jax.shard_map(
        functools.partial(on_device, ring, n_chan),
        mesh=split,
        in_specs=placed,
        out_specs=P(tok, chan),
        check_vma=False,
    )
```

```python
import functools

import jax
import jax.numpy as jnp
from jax import lax
from jax.experimental import pallas as pl
from jax.experimental.pallas import tpu as pltpu
from jax.sharding import Mesh
from jax.sharding import PartitionSpec as P

LANES = 128
EPSILON = 1e-05
VMEM_BYTES = 48 * 1024 * 1024

BRIEF = pl.CostEstimate(flops=1024, bytes_accessed=1024, transcendentals=0)

SWAP = [(1, 2), (2, 1)]
CYCLE = [(0, 2), (1, 0), (2, 3), (3, 1)]
PAIR = [(0, 1), (1, 0)]


def fence(*blocks):
    return lax.optimization_barrier(blocks)


def params(parallel):
    return pltpu.CompilerParams(
        dimension_semantics=("arbitrary",) * parallel, vmem_limit_bytes=VMEM_BYTES
    )


def toeplitz_into(table_ref, base_ref, taps, count):
    for q in range(count):
        row = jnp.broadcast_to(base_ref[q : q + 1, :], (taps, 2 * taps))
        band = pltpu.roll(row, 0, 1, stride=1, stride_axis=0)
        table_ref[q * taps : (q + 1) * taps, :] = band.astype(table_ref.dtype)


def banded(table, keep, source, taps, count):
    table = table.reshape(count, taps, 2 * taps)
    masked = (table * keep[None]).reshape(count * taps, 2 * taps)
    wide = jnp.dot(masked, source, preferred_element_type=jnp.float32)
    width = source.shape[1]
    owner = lax.broadcasted_iota(jnp.int32, (taps, width), 1) // (width // count)
    total = wide[:taps]
    for q in range(1, count):
        total = jnp.where(owner == q, wide[q * taps : (q + 1) * taps], total)
    return total


def forward_kernel(
    taps, count, base_ref, last_ref, tail_ref, keys_ref, values_ref, mix_ref, conv_ref,
    q_ref, k_ref, table_ref, source_ref,
):
    rows, width = keys_ref.shape
    parts = width // LANES
    toeplitz_into(table_ref, base_ref, taps, parts * count)
    values = values_ref[...].astype(jnp.float32)
    source_ref[:taps, :] = tail_ref[...]
    source_ref[taps:, :] = (keys_ref[...].astype(jnp.float32) * values).astype(jnp.bfloat16)
    k_ref[...] = (conv_ref[...] * values).astype(k_ref.dtype)

    def tile(i, carry):
        row = pl.multiple_of(i * taps, taps)
        col = lax.broadcasted_iota(jnp.int32, (taps, 2 * taps), 1) + (i - 1) * taps
        keep = jnp.where(col >= last_ref[pl.ds(row, taps), :], 1.0, 0.0).astype(jnp.bfloat16)
        for p in range(parts):
            lanes = slice(p * LANES, (p + 1) * LANES)
            table = table_ref[p * count * taps : (p + 1) * count * taps, :]
            mixed = banded(table, keep, source_ref[pl.ds(row, 2 * taps), lanes], taps, count)
            at = (pl.ds(row, taps), lanes)
            q_ref[at] = (mix_ref[at] * mixed).astype(q_ref.dtype)
        return carry

    lax.fori_loop(0, rows // taps, tile, 0)


def backward_kernel(
    taps, count, base_ref, last_ref, head_ref, keys_ref, queries_ref, mix_ref,
    conv_ref, v_ref, table_ref, source_ref,
):
    rows, width = keys_ref.shape
    parts = width // LANES
    toeplitz_into(table_ref, base_ref, taps, parts * count)
    source_ref[:rows, :] = (mix_ref[...] * queries_ref[...].astype(jnp.float32)).astype(jnp.bfloat16)
    source_ref[rows:, :] = head_ref[...]

    def tile(i, carry):
        row = pl.multiple_of(i * taps, taps)
        at_row = lax.broadcasted_iota(jnp.int32, (taps, 2 * taps), 0) + i * taps
        keep = jnp.where(at_row >= last_ref[:, pl.ds(row, 2 * taps)], 1.0, 0.0).astype(jnp.bfloat16)
        for p in range(parts):
            lanes = slice(p * LANES, (p + 1) * LANES)
            table = table_ref[p * count * taps : (p + 1) * count * taps, :]
            conv = banded(table, keep, source_ref[pl.ds(row, 2 * taps), lanes], taps, count)
            at = (pl.ds(row, taps), lanes)
            conv_ref[at] = conv
            v_ref[at] = (conv * keys_ref[at].astype(jnp.float32)).astype(v_ref.dtype)
        return carry

    lax.fori_loop(0, rows // taps, tile, 0)


def conv_call(kernel, name, base, last, edge, operands, dtypes, taps, per):
    rows, width = operands[0].shape
    cols = min(width, 4 * LANES)
    count = cols // LANES * per
    slab = pl.BlockSpec((rows, cols), lambda g: (0, g))
    return pl.pallas_call(
        functools.partial(kernel, taps, per),
        grid=(width // cols,),
        in_specs=[
            pl.BlockSpec((count, 2 * taps), lambda g: (g, 0)),
            pl.BlockSpec(last.shape, lambda g: (0, 0)),
            pl.BlockSpec((taps, cols), lambda g: (0, g)),
        ]
        + [slab] * len(operands),
        out_specs=[slab] * len(dtypes),
        out_shape=[jax.ShapeDtypeStruct((rows, width), t) for t in dtypes],
        scratch_shapes=[
            pltpu.VMEM((count * taps, 2 * taps), jnp.bfloat16),
            pltpu.VMEM((rows + taps, cols), jnp.bfloat16),
        ],
        compiler_params=params(1),
        cost_estimate=BRIEF,
        name=name,
    )(base, last, edge, *operands)


NT = (((1,), (1,)), ((), ()))


def mix_kernel(at_ref, *refs):
    lefts, own_ref, sib_ref, out_ref = refs[:-3], *refs[-3:]
    step = pl.program_id(1)
    both = None
    for n, left in enumerate(lefts):
        right = (own_ref, sib_ref)[n % 2][n // 2]
        part = lax.dot_general(left[...], right, NT, preferred_element_type=jnp.float32)
        both = part if both is None else both + part

    @pl.when(step == 0)
    def _():
        out_ref[...] = both

    @pl.when(step > 0)
    def _():
        out_ref[...] += both


def mix_matmul(at, grads, own, sib):
    rows = grads.shape[0]
    blocks, width, feats = own.shape
    cols = min(width, 1024)
    lefts = [
        pl.BlockSpec((rows, feats), lambda n, j, at, side=side, k=k: (0, at[side, 2 * j + k]))
        for k in range(2)
        for side in range(2)
    ]
    right = pl.BlockSpec((2, cols, feats), lambda n, j, at: (j, n, 0))
    return pl.pallas_call(
        mix_kernel,
        grid_spec=pltpu.PrefetchScalarGridSpec(
            num_scalar_prefetch=1,
            grid=(width // cols, blocks // 2),
            in_specs=lefts + [right, right],
            out_specs=pl.BlockSpec((rows, cols), lambda n, j, at: (0, n)),
        ),
        out_shape=jax.ShapeDtypeStruct((rows, width), jnp.float32),
        compiler_params=params(2),
        cost_estimate=BRIEF,
        name="mix_matmul",
    )(at, *[grads] * len(lefts), own, sib)


def project_kernel(places, blocks, *refs):
    half = pl.num_programs(0) // 2
    own, sib = refs[: len(places)], refs[len(places) : 2 * len(places)]
    weights, outs = refs[2 * len(places) : -2], refs[-2:]

    def into(grads, out_ref):
        for n in range(blocks):
            total = None
            for grad, (b, left) in zip(grads, places):
                right = weights[n][b, :, left : left + grad.shape[1]]
                part = lax.dot_general(grad[...], right, NT, preferred_element_type=jnp.float32)
                total = part if total is None else total + part
            out_ref[n] = total.astype(out_ref.dtype)

    @pl.when(pl.program_id(0) < half)
    def _():
        into(own, outs[0])

    @pl.when(pl.program_id(0) >= half)
    def _():
        into(sib, outs[1])


def project(own, sib, weights):
    blocks = len(weights)
    branches, feats, width = weights[0].shape
    rows = own[0][0].shape[0]
    places = [
        (b, sum(p.shape[1] for p in pieces[:at])) for b, pieces in enumerate(own) for at in range(len(pieces))
    ]
    own, sib = [p for pieces in own for p in pieces], [p for pieces in sib for p in pieces]
    half = 2
    step = rows // half

    def first(i):
        return jnp.minimum(i, half - 1)

    def second(i):
        return jnp.maximum(i - half, 0)

    out = jax.ShapeDtypeStruct((blocks, rows, feats), jnp.bfloat16)
    return pl.pallas_call(
        functools.partial(project_kernel, places, blocks),
        grid=(2 * half,),
        in_specs=[pl.BlockSpec((step, p.shape[1]), lambda i: (first(i), 0)) for p in own]
        + [pl.BlockSpec((step, p.shape[1]), lambda i: (second(i), 0)) for p in sib]
        + [pl.BlockSpec((branches, feats, width), lambda i: (0, 0, 0))] * blocks,
        out_specs=[
            pl.BlockSpec((blocks, step, feats), lambda i: (0, first(i), 0)),
            pl.BlockSpec((blocks, step, feats), lambda i: (0, second(i), 0)),
        ],
        out_shape=[out, out],
        compiler_params=params(1),
        cost_estimate=BRIEF,
        name="project",
    )(*own, *sib, *weights)


def pick_kernel(at_ref, own_ref, sib_ref, input_ref, gain_ref, norm_ref, cross_ref):
    step = pl.program_id(0)
    ours = (lax.broadcasted_iota(jnp.int32, own_ref.shape[1:], 0) * 0 + at_ref[2, step]) == 1
    norm = jnp.where(ours, own_ref[0].astype(jnp.float32), sib_ref[0].astype(jnp.float32))
    norm_ref[...] = norm.astype(norm_ref.dtype)
    part = jnp.sum(
        gain_ref[...].astype(jnp.float32) * norm * input_ref[...].astype(jnp.float32),
        axis=1,
        keepdims=True,
    )

    @pl.when(step == 0)
    def _():
        cross_ref[...] = part

    @pl.when(step > 0)
    def _():
        cross_ref[...] += part


def pick(at, own, sib, block_input, gain):
    rows, width = block_input.shape
    feats = own.shape[2]
    return pl.pallas_call(
        pick_kernel,
        grid_spec=pltpu.PrefetchScalarGridSpec(
            num_scalar_prefetch=1,
            grid=(width // feats,),
            in_specs=[
                pl.BlockSpec((1, rows, feats), lambda j, at: (at[0, j], 0, 0)),
                pl.BlockSpec((1, rows, feats), lambda j, at: (at[1, j], 0, 0)),
                pl.BlockSpec((rows, feats), lambda j, at: (0, j)),
                pl.BlockSpec((1, feats), lambda j, at: (0, j)),
            ],
            out_specs=[
                pl.BlockSpec((rows, feats), lambda j, at: (0, j)),
                pl.BlockSpec((rows, 1), lambda j, at: (0, 0)),
            ],
        ),
        out_shape=[
            jax.ShapeDtypeStruct((rows, width), jnp.bfloat16),
            jax.ShapeDtypeStruct((rows, 1), jnp.float32),
        ],
        compiler_params=params(1),
        cost_estimate=BRIEF,
        name="pick",
    )(at, own, sib, block_input, gain)


def on_device(
    ring,
    n_chan,
    grad_out,
    block_input,
    norm_gain,
    queries,
    keys,
    values,
    filters,
    doc_starts,
    in_weight,
    out_weight,
):
    rows, width = grad_out.shape
    groups, taps = filters.shape
    feats, branches = in_weight.shape[:2]
    count = len(ring)
    per = LANES * groups // width
    features = feats * 2 * count
    o, x, h, c = (lax.axis_index(a) for a in ("o", "x", "h", "c"))
    order = jnp.array(ring, jnp.int32)
    place = jnp.array([ring.index(i) for i in range(count)], jnp.int32)
    position = place[o]
    far = count // 2
    forth = [(ring[i], ring[(i + 1) % count]) for i in range(count)]
    back = [(b, a) for a, b in forth]

    def exchanged(block):
        return lax.ppermute(block, ("x", "c"), SWAP)

    def swapped(block):
        return jnp.where(x == c, block, exchanged(block))

    def sibling(block):
        return lax.ppermute(block, "c", PAIR)

    def both_ways(up, down):
        return lax.ppermute(up, ("o",), forth), lax.ppermute(down, ("o",), back)

    def far_halves(up, down, axis):
        half = up.shape[axis] // 2
        return both_ways(
            lax.slice_in_dim(up, 0, half, axis=axis),
            lax.slice_in_dim(down, half, 2 * half, axis=axis),
        )

    all_starts = lax.all_gather(doc_starts, ("o", "x"), axis=0, tiled=True)
    taps32 = swapped(filters).astype(jnp.float32)
    out_w = swapped(out_weight)
    in_w = jnp.swapaxes(in_weight, 0, 1)
    out_w, in_w, grad_out, taps32 = fence(out_w, in_w, grad_out, taps32)

    in_recv = exchanged(in_w)
    blocks = [out_w]
    up = down = out_w
    for s in range(1, far):
        up, down = both_ways(up, down)
        if s == far - 2:
            up, down, in_recv, in_w, grad_out = fence(up, down, in_recv, in_w, grad_out)
        blocks += [up, down]
    in_w = jnp.where(x == c, in_w, in_recv)
    half_recv = exchanged(grad_out)
    blocks.append(jnp.concatenate(far_halves(up, down, 0), axis=0))
    own_out = jnp.stack(blocks)
    source_in = block_input.astype(jnp.float32)
    square_sum = jnp.sum(source_in * source_in, axis=1, keepdims=True)
    distances = [0] + [d for s in range(1, far) for d in (-s, s)] + [far]
    sources = order[(position + jnp.array(distances, jnp.int32)) % count]
    wide = width // feats

    def column(parity):
        block = sources * 2 + parity
        owner = block // wide
        side = jnp.where(owner % 2 == x, 0, 1)
        return side * (n_chan * wide) + (owner // 2) * wide + block % wide

    columns = jnp.stack([column(c), column(1 - c)])
    slabs = 2 * count
    slab = o * 2 + c
    onward = [(i, i + 1) for i in range(slabs - 1)]
    backward = [(i + 1, i) for i in range(slabs - 1)]
    positions = jnp.arange(rows, dtype=jnp.int32)

    def last_of(at):
        starts = all_starts[jnp.minimum(at, slabs - 1)]
        prior = jnp.where(at > 0, all_starts[jnp.maximum(at - 1, 0), -1], 0)
        own = jnp.where(starts[None, :] <= positions[:, None], starts[None, :], -rows)
        return jnp.maximum(jnp.max(own, axis=1), prior - rows)

    last_start = last_of(slab)
    padded_last = jnp.concatenate([last_start, last_of(slab + 1)[:taps] + rows])[None]
    edge = jnp.zeros((groups, taps), jnp.float32)
    base_back = jnp.concatenate([taps32, edge], axis=1)
    base_fore = jnp.concatenate([edge[:, :1], taps32[:, ::-1], edge[:, 1:]], axis=1)
    own_out, in_w, half_recv, grad_out, square_sum, padded_last, last_col, base_back, base_fore, columns = fence(
        own_out, in_w, half_recv, grad_out, square_sum, padded_last, last_start[:, None], base_back,
        base_fore, columns,
    )

    ahead, behind = {0: in_w}, {0: in_w}
    ahead[1], behind[1] = both_ways(in_w, in_w)
    sib_out = sibling(own_out)
    grad_other = lax.ppermute(grad_out, ("x", "c"), CYCLE)
    grad_other, keys = fence(grad_other, keys)
    k_recv = exchanged(keys)
    grad_half = jnp.where(x == c, grad_out, half_recv)
    if n_chan > 1:
        grad_half = lax.all_gather(grad_half, "h", axis=1, tiled=True)
        grad_other = lax.all_gather(grad_other, "h", axis=1, tiled=True)
    grads = jnp.concatenate([grad_half, grad_other], axis=1)
    mix_grad = mix_matmul(columns, grads, own_out, sib_out)
    ahead[1], behind[1], mix_grad, k_recv, queries = fence(
        ahead[1], behind[1], mix_grad, k_recv, queries
    )

    ahead[2], behind[2] = both_ways(ahead[1], behind[1])
    q_recv, queries, values, mix_grad = fence(exchanged(queries), queries, values, mix_grad)
    middle = width // 2
    parts = (slice(0, middle), slice(middle, width))
    v_recv = exchanged(values[:, parts[0]])
    own_k, own_q = jnp.where(x == c, keys, k_recv), jnp.where(x == c, queries, q_recv)
    head = (mix_grad[:taps] * own_q[:taps].astype(jnp.float32)).astype(jnp.bfloat16)
    head = lax.ppermute(head, ("o", "c"), backward)
    conv, v_grad = conv_call(
        backward_kernel, "backward_conv", base_back, padded_last, head,
        [own_k, own_q, mix_grad], [jnp.float32, jnp.bfloat16], taps, per,
    )
    v_recv, values, conv, v_grad = fence(v_recv, values, conv, v_grad)

    def forward(at, received):
        own_v = jnp.where(x == c, values[:, parts[at]], received)
        part_k = own_k[:, parts[at]]
        tail = part_k[rows - taps :].astype(jnp.float32) * own_v[rows - taps :].astype(jnp.float32)
        tail = lax.ppermute(tail.astype(jnp.bfloat16), ("o", "c"), onward)
        base = base_fore[at * groups // 2 : (at + 1) * groups // 2]
        return conv_call(
            forward_kernel, "forward_conv", base, last_col, tail,
            [part_k, own_v, mix_grad[:, parts[at]], conv[:, parts[at]]],
            [jnp.bfloat16, jnp.bfloat16], taps, per,
        )

    later = exchanged(values[:, parts[1]])
    q_left, k_left = forward(0, v_recv)
    sib_v = sibling(v_grad)
    ahead[2], behind[2], q_left, k_left, later, v_grad = fence(
        ahead[2], behind[2], q_left, k_left, later, v_grad
    )

    ahead[3], behind[3] = both_ways(ahead[2], behind[2])
    q_right, k_right = forward(1, later)
    own_grads = [[q_left, q_right], [k_left, k_right], [v_grad]]
    sib_grads = [[sibling(p) for p in pieces] for pieces in own_grads[:2]] + [[sib_v]]

    norms = []

    def add_blocks(weights):
        ours, theirs = project(own_grads, sib_grads, weights)
        keep = jnp.where(c == x, ours, theirs)
        send = jnp.where(c == x, theirs, ours)
        received = lax.ppermute(send, "x", PAIR)
        norms.append((keep.astype(jnp.float32) + received.astype(jnp.float32)).astype(jnp.bfloat16))

    for s in range(3, far + 1):
        if 3 < s < far:
            ahead[s], behind[s] = both_ways(ahead[s - 1], behind[s - 1])
        elif s == far:
            up, down = far_halves(ahead[s - 1], behind[s - 1], 1)
        if s == 3:
            add_blocks([in_w, ahead[1], behind[1]])
        add_blocks([ahead[s - 1], behind[s - 1]])
        if s < far:
            ahead[s], behind[s], norms[-1] = fence(ahead[s], behind[s], norms[-1])
        else:
            up, down, norms[-1] = fence(up, down, norms[-1])
    add_blocks([jnp.concatenate([up, down], axis=1)])
    if n_chan > 1:
        norm = jnp.concatenate(norms, axis=0)
        slot = jnp.zeros((count,), jnp.int32).at[sources].set(jnp.arange(count, dtype=jnp.int32))
        norm = lax.psum_scatter(
            jnp.take(norm, slot, axis=0), "h", scatter_dimension=0, tiled=True
        )
        other = lax.ppermute(norm, "c", PAIR)
        slot = jnp.arange(count, dtype=jnp.int32) - h * (count // n_chan)
    else:
        norm = jnp.concatenate(norms, axis=0)
        other = jnp.concatenate([lax.ppermute(n, "c", PAIR) for n in norms], axis=0)
        slot = jnp.zeros((count,), jnp.int32).at[sources].set(jnp.arange(count, dtype=jnp.int32))
    mine = (h * 2 + c) * wide + jnp.arange(wide, dtype=jnp.int32)
    slots = slot[mine // 2]
    at = jnp.stack([slots, slots, (mine % 2 == c).astype(jnp.int32)])
    norm_grad, cross = pick(at, norm, other, block_input, norm_gain[None])
    cross_sum, square_sum = lax.psum((cross, square_sum), ("h", "c"))
    inverse = lax.rsqrt(square_sum / features + EPSILON)
    scaled = norm_gain.astype(jnp.float32)[None, :] * norm_grad.astype(jnp.float32)
    result = (
        grad_out.astype(jnp.float32)
        + inverse * scaled
        - source_in * (inverse * inverse * inverse) * cross_sum / features
    )
    return result.astype(jnp.bfloat16)


def solution(mesh):
    outer, n_chan = mesh.shape["ctx"] // 2, mesh.shape["ch"] // 2
    split = Mesh(mesh.devices.reshape(outer, 2, n_chan, 2), ("o", "x", "h", "c"))
    ring = list(range(0, outer, 2)) + list(range(outer - 1, 0, -2))
    tok, chan = ("o", "x"), ("h", "c")
    placed = (
        P(tok, chan),
        P(tok, chan),
        P(chan),
        P(tok, chan),
        P(tok, chan),
        P(tok, chan),
        P(chan, None),
        P(tok, None),
        P(tok, None, chan),
        P(chan, tok),
    )
    return jax.shard_map(
        functools.partial(on_device, ring, n_chan),
        mesh=split,
        in_specs=placed,
        out_specs=P(tok, chan),
        check_vma=False,
    )
```

```python
import functools

import jax
import jax.numpy as jnp
from jax import lax
from jax.experimental import pallas as pl
from jax.experimental.pallas import tpu as pltpu
from jax.sharding import Mesh
from jax.sharding import PartitionSpec as P

LANES = 128
EPSILON = 1e-05
VMEM_BYTES = 52 * 1024 * 1024

BRIEF = pl.CostEstimate(flops=1024, bytes_accessed=1024, transcendentals=0)

SWAP = [(1, 2), (2, 1)]
CYCLE = [(0, 2), (1, 0), (2, 3), (3, 1)]
PAIR = [(0, 1), (1, 0)]


def fence(*blocks):
    return lax.optimization_barrier(blocks)


def params(parallel):
    return pltpu.CompilerParams(
        dimension_semantics=("arbitrary",) * parallel, vmem_limit_bytes=VMEM_BYTES
    )


def toeplitz_into(table_ref, base_ref, taps, count):
    for q in range(count):
        row = jnp.broadcast_to(base_ref[q : q + 1, :], (taps, 2 * taps))
        band = pltpu.roll(row, 0, 1, stride=1, stride_axis=0)
        table_ref[q * taps : (q + 1) * taps, :] = band.astype(table_ref.dtype)


def banded(table, keep, source, taps, count):
    table = table.reshape(count, taps, 2 * taps)
    masked = (table * keep[None]).reshape(count * taps, 2 * taps)
    wide = jnp.dot(masked, source, preferred_element_type=jnp.float32)
    width = source.shape[1]
    owner = lax.broadcasted_iota(jnp.int32, (taps, width), 1) // (width // count)
    total = wide[:taps]
    for q in range(1, count):
        total = jnp.where(owner == q, wide[q * taps : (q + 1) * taps], total)
    return total


def forward_kernel(
    taps, count, base_ref, last_ref, tail_ref, keys_ref, values_ref, mix_ref, conv_ref,
    q_ref, k_ref, table_ref, source_ref,
):
    rows, width = keys_ref.shape
    parts = width // LANES
    toeplitz_into(table_ref, base_ref, taps, parts * count)
    values = values_ref[...].astype(jnp.float32)
    source_ref[:taps, :] = tail_ref[...]
    source_ref[taps:, :] = (keys_ref[...].astype(jnp.float32) * values).astype(jnp.bfloat16)
    k_ref[...] = (conv_ref[...] * values).astype(k_ref.dtype)

    def tile(i, carry):
        row = pl.multiple_of(i * taps, taps)
        col = lax.broadcasted_iota(jnp.int32, (taps, 2 * taps), 1) + (i - 1) * taps
        keep = jnp.where(col >= last_ref[pl.ds(row, taps), :], 1.0, 0.0).astype(jnp.bfloat16)
        for p in range(parts):
            lanes = slice(p * LANES, (p + 1) * LANES)
            table = table_ref[p * count * taps : (p + 1) * count * taps, :]
            mixed = banded(table, keep, source_ref[pl.ds(row, 2 * taps), lanes], taps, count)
            at = (pl.ds(row, taps), lanes)
            q_ref[at] = (mix_ref[at] * mixed).astype(q_ref.dtype)
        return carry

    lax.fori_loop(0, rows // taps, tile, 0)


def backward_kernel(
    taps, count, base_ref, last_ref, keys_ref, queries_ref, mix_ref,
    conv_ref, v_ref, table_ref, source_ref,
):
    rows, width = keys_ref.shape
    parts = width // LANES
    toeplitz_into(table_ref, base_ref, taps, parts * count)
    source_ref[:rows, :] = (mix_ref[...] * queries_ref[...].astype(jnp.float32)).astype(jnp.bfloat16)

    def tile(i, carry):
        row = pl.multiple_of(i * taps, taps)
        at_row = lax.broadcasted_iota(jnp.int32, (taps, 2 * taps), 0) + i * taps
        keep = jnp.where(at_row >= last_ref[:, pl.ds(row, 2 * taps)], 1.0, 0.0).astype(jnp.bfloat16)
        for p in range(parts):
            lanes = slice(p * LANES, (p + 1) * LANES)
            table = table_ref[p * count * taps : (p + 1) * count * taps, :]
            conv = banded(table, keep, source_ref[pl.ds(row, 2 * taps), lanes], taps, count)
            at = (pl.ds(row, taps), lanes)
            conv_ref[at] = conv
            v_ref[at] = (conv * keys_ref[at].astype(jnp.float32)).astype(v_ref.dtype)
        return carry

    lax.fori_loop(0, rows // taps - 1, tile, 0)


def ending_kernel(
    taps, count, base_ref, last_ref, head_ref, keys_ref, queries_ref, mix_ref, conv_in, v_in,
    conv_ref, v_ref, table_ref,
):
    del conv_in, v_in
    rows = last_ref.shape[1] - taps
    parts = keys_ref.shape[1] // LANES
    toeplitz_into(table_ref, base_ref, taps, parts * count)
    current = (mix_ref[...] * queries_ref[...].astype(jnp.float32)).astype(jnp.bfloat16)
    source = jnp.concatenate([current, head_ref[...]], axis=0)
    at_row = lax.broadcasted_iota(jnp.int32, (taps, 2 * taps), 0) + rows - taps
    keep = jnp.where(at_row >= last_ref[:, rows - taps :], 1.0, 0.0).astype(jnp.bfloat16)
    for p in range(parts):
        lanes = slice(p * LANES, (p + 1) * LANES)
        table = table_ref[p * count * taps : (p + 1) * count * taps, :]
        conv = banded(table, keep, source[:, lanes], taps, count)
        conv_ref[:, lanes] = conv
        v_ref[:, lanes] = (conv * keys_ref[:, lanes].astype(jnp.float32)).astype(v_ref.dtype)


def conv_call(kernel, name, base, last, edge, operands, dtypes, taps, per, width, start=0):
    rows = operands[0].shape[0]
    cols = min(width, 4 * LANES)
    count = cols // LANES * per
    skip = start // cols

    def offset(whole):
        return skip if whole != width else 0

    edges = [] if edge is None else [edge]
    ahead = skip
    return pl.pallas_call(
        functools.partial(kernel, taps, per),
        grid=(width // cols,),
        in_specs=[
            pl.BlockSpec((count, 2 * taps), lambda g: (g + ahead, 0)),
            pl.BlockSpec(last.shape, lambda g: (0, 0)),
        ]
        + [pl.BlockSpec((taps, cols), lambda g: (0, g + ahead))] * len(edges)
        + [
            pl.BlockSpec((rows, cols), lambda g, d=offset(operand.shape[1]): (0, g + d))
            for operand in operands
        ],
        out_specs=[pl.BlockSpec((rows, cols), lambda g: (0, g))] * len(dtypes),
        out_shape=[jax.ShapeDtypeStruct((rows, width), t) for t in dtypes],
        scratch_shapes=[
            pltpu.VMEM((count * taps, 2 * taps), jnp.bfloat16),
            pltpu.VMEM((rows + taps, cols), jnp.bfloat16),
        ],
        compiler_params=params(1),
        cost_estimate=BRIEF,
        name=name,
    )(base, last, *edges, *operands)


def ending_call(base, last, head, operands, conv, grad, taps, per):
    rows, width = conv.shape
    cols = min(width, 4 * LANES)
    count = cols // LANES * per
    tile = pl.BlockSpec((taps, cols), lambda g: (rows // taps - 1, g))
    whole = pl.BlockSpec(memory_space=pl.ANY)
    return pl.pallas_call(
        functools.partial(ending_kernel, taps, per),
        grid=(width // cols,),
        in_specs=[
            pl.BlockSpec((count, 2 * taps), lambda g: (g, 0)),
            pl.BlockSpec(last.shape, lambda g: (0, 0)),
            pl.BlockSpec((taps, cols), lambda g: (0, g)),
            tile, tile, tile, whole, whole,
        ],
        out_specs=[tile, tile],
        out_shape=[jax.ShapeDtypeStruct(a.shape, a.dtype) for a in (conv, grad)],
        scratch_shapes=[pltpu.VMEM((count * taps, 2 * taps), jnp.bfloat16)],
        input_output_aliases={6: 0, 7: 1},
        compiler_params=params(1),
        cost_estimate=BRIEF,
        name="backward_ending",
    )(base, last, head, *operands, conv, grad)


NT = (((1,), (1,)), ((), ()))


def mix_kernel(at_ref, *refs):
    lefts, own_ref, sib_ref, out_ref = refs[:-3], *refs[-3:]
    step = pl.program_id(1)
    both = None
    for n, left in enumerate(lefts):
        right = (own_ref, sib_ref)[n % 2][n // 2]
        part = lax.dot_general(left[...], right, NT, preferred_element_type=jnp.float32)
        both = part if both is None else both + part

    @pl.when(step == 0)
    def _():
        out_ref[...] = both

    @pl.when(step > 0)
    def _():
        out_ref[...] += both


def mix_matmul(at, grads, own, sib):
    rows = grads.shape[0]
    blocks, width, feats = own.shape
    cols = min(width, 1024)
    lefts = [
        pl.BlockSpec((rows, feats), lambda n, j, at, side=side, k=k: (0, at[side, 2 * j + k]))
        for k in range(2)
        for side in range(2)
    ]
    right = pl.BlockSpec((2, cols, feats), lambda n, j, at: (j, n, 0))
    return pl.pallas_call(
        mix_kernel,
        grid_spec=pltpu.PrefetchScalarGridSpec(
            num_scalar_prefetch=1,
            grid=(width // cols, blocks // 2),
            in_specs=lefts + [right, right],
            out_specs=pl.BlockSpec((rows, cols), lambda n, j, at: (0, n)),
        ),
        out_shape=jax.ShapeDtypeStruct((rows, width), jnp.float32),
        compiler_params=params(2),
        cost_estimate=BRIEF,
        name="mix_matmul",
    )(at, *[grads] * len(lefts), own, sib)


def project_kernel(places, blocks, *refs):
    half = pl.num_programs(0) // 2
    own, sib = refs[: len(places)], refs[len(places) : 2 * len(places)]
    weights, outs = refs[2 * len(places) : -2], refs[-2:]

    def into(grads, out_ref):
        for n in range(blocks):
            total = None
            for grad, (b, left) in zip(grads, places):
                right = weights[n][b, :, left : left + grad.shape[1]]
                part = lax.dot_general(grad[...], right, NT, preferred_element_type=jnp.float32)
                total = part if total is None else total + part
            out_ref[n] = total.astype(out_ref.dtype)

    @pl.when(pl.program_id(0) < half)
    def _():
        into(own, outs[0])

    @pl.when(pl.program_id(0) >= half)
    def _():
        into(sib, outs[1])


def project(own, sib, weights):
    blocks = len(weights)
    branches, feats, width = weights[0].shape
    rows = own[0][0].shape[0]
    places = [
        (b, sum(p.shape[1] for p in pieces[:at])) for b, pieces in enumerate(own) for at in range(len(pieces))
    ]
    own, sib = [p for pieces in own for p in pieces], [p for pieces in sib for p in pieces]
    half = 2
    step = rows // half

    def first(i):
        return jnp.minimum(i, half - 1)

    def second(i):
        return jnp.maximum(i - half, 0)

    out = jax.ShapeDtypeStruct((blocks, rows, feats), jnp.bfloat16)
    return pl.pallas_call(
        functools.partial(project_kernel, places, blocks),
        grid=(2 * half,),
        in_specs=[pl.BlockSpec((step, p.shape[1]), lambda i: (first(i), 0)) for p in own]
        + [pl.BlockSpec((step, p.shape[1]), lambda i: (second(i), 0)) for p in sib]
        + [
            pl.BlockSpec((branches, feats, width), lambda i: (0, 0, 0), pipeline_mode=pl.Buffered(1))
        ]
        * blocks,
        out_specs=[
            pl.BlockSpec((blocks, step, feats), lambda i: (0, first(i), 0)),
            pl.BlockSpec((blocks, step, feats), lambda i: (0, second(i), 0)),
        ],
        out_shape=[out, out],
        compiler_params=params(1),
        cost_estimate=BRIEF,
        name="project",
    )(*own, *sib, *weights)


def pick_kernel(at_ref, own_ref, sib_ref, input_ref, gain_ref, norm_ref, cross_ref):
    step = pl.program_id(0)
    ours = (lax.broadcasted_iota(jnp.int32, own_ref.shape[1:], 0) * 0 + at_ref[2, step]) == 1
    norm = jnp.where(ours, own_ref[0].astype(jnp.float32), sib_ref[0].astype(jnp.float32))
    norm_ref[...] = norm.astype(norm_ref.dtype)
    part = jnp.sum(
        gain_ref[...].astype(jnp.float32) * norm * input_ref[...].astype(jnp.float32),
        axis=1,
        keepdims=True,
    )

    @pl.when(step == 0)
    def _():
        cross_ref[...] = part

    @pl.when(step > 0)
    def _():
        cross_ref[...] += part


def pick(at, own, sib, block_input, gain):
    rows, width = block_input.shape
    feats = own.shape[2]
    return pl.pallas_call(
        pick_kernel,
        grid_spec=pltpu.PrefetchScalarGridSpec(
            num_scalar_prefetch=1,
            grid=(width // feats,),
            in_specs=[
                pl.BlockSpec((1, rows, feats), lambda j, at: (at[0, j], 0, 0)),
                pl.BlockSpec((1, rows, feats), lambda j, at: (at[1, j], 0, 0)),
                pl.BlockSpec((rows, feats), lambda j, at: (0, j)),
                pl.BlockSpec((1, feats), lambda j, at: (0, j)),
            ],
            out_specs=[
                pl.BlockSpec((rows, feats), lambda j, at: (0, j)),
                pl.BlockSpec((rows, 1), lambda j, at: (0, 0)),
            ],
        ),
        out_shape=[
            jax.ShapeDtypeStruct((rows, width), jnp.bfloat16),
            jax.ShapeDtypeStruct((rows, 1), jnp.float32),
        ],
        compiler_params=params(1),
        cost_estimate=BRIEF,
        name="pick",
    )(at, own, sib, block_input, gain)


def on_device(
    ring,
    n_chan,
    grad_out,
    block_input,
    norm_gain,
    queries,
    keys,
    values,
    filters,
    doc_starts,
    in_weight,
    out_weight,
):
    rows, width = grad_out.shape
    groups, taps = filters.shape
    feats, branches = in_weight.shape[:2]
    count = len(ring)
    per = LANES * groups // width
    features = feats * 2 * count
    o, x, h, c = (lax.axis_index(a) for a in ("o", "x", "h", "c"))
    order = jnp.array(ring, jnp.int32)
    place = jnp.array([ring.index(i) for i in range(count)], jnp.int32)
    position = place[o]
    far = count // 2
    forth = [(ring[i], ring[(i + 1) % count]) for i in range(count)]
    back = [(b, a) for a, b in forth]

    def exchanged(block):
        return lax.ppermute(block, ("x", "c"), SWAP)

    def swapped(block):
        return jnp.where(x == c, block, exchanged(block))

    def sibling(block):
        return lax.ppermute(block, "c", PAIR)

    def both_ways(up, down):
        return lax.ppermute(up, ("o",), forth), lax.ppermute(down, ("o",), back)

    def far_halves(up, down, axis):
        half = up.shape[axis] // 2
        return both_ways(
            lax.slice_in_dim(up, 0, half, axis=axis),
            lax.slice_in_dim(down, half, 2 * half, axis=axis),
        )

    def neighbour(block, distance):
        route = []
        for i in range(count):
            for core in range(2):
                source = i * 2 + core + distance
                if 0 <= source < 2 * count:
                    route += [(source * 2 + side, (i * 2 + side) * 2 + core) for side in range(2)]
        return lax.ppermute(block, ("o", "x", "c"), route)

    starts = swapped(doc_starts)[0]
    prior = neighbour(doc_starts, -1)[0, -1]
    following = neighbour(doc_starts, 1)[0]
    tail = (keys[rows - taps :].astype(jnp.float32) * values[rows - taps :].astype(jnp.float32)).astype(
        jnp.bfloat16
    )
    taps32 = swapped(filters).astype(jnp.float32)
    out_w = swapped(out_weight)
    in_w = jnp.swapaxes(in_weight, 0, 1)
    out_w, in_w, grad_out, taps32, starts, prior, following, tail = fence(
        out_w, in_w, grad_out, taps32, starts, prior, following, tail
    )

    in_recv, half_recv = exchanged(in_w), exchanged(grad_out)
    tail = neighbour(tail, -1)
    blocks = [out_w]
    up = down = out_w
    for s in range(1, far):
        up, down = both_ways(up, down)
        if s == far - 1:
            up, down, in_recv, in_w, half_recv, grad_out, tail = fence(
                up, down, in_recv, in_w, half_recv, grad_out, tail
            )
        blocks += [up, down]
    in_w = jnp.where(x == c, in_w, in_recv)
    spans = (slice(0, rows // 2), slice(rows // 2, rows))
    other_up = lax.ppermute(grad_out[spans[0]], ("x", "c"), CYCLE)
    grad_half = jnp.where(x == c, grad_out, half_recv)
    blocks.append(jnp.concatenate(far_halves(up, down, 0), axis=0))
    own_out = jnp.stack(blocks)
    source_in = block_input.astype(jnp.float32)
    square_sum = jnp.sum(source_in * source_in, axis=1, keepdims=True)
    distances = [0] + [d for s in range(1, far) for d in (-s, s)] + [far]
    sources = order[(position + jnp.array(distances, jnp.int32)) % count]
    wide = width // feats

    def column(parity):
        block = sources * 2 + parity
        owner = block // wide
        side = jnp.where(owner % 2 == x, 0, 1)
        return side * (n_chan * wide) + (owner // 2) * wide + block % wide

    columns = jnp.stack([column(c), column(1 - c)])
    slabs = 2 * count
    backward = [(i + 1, i) for i in range(slabs - 1)]
    positions = jnp.arange(rows, dtype=jnp.int32)

    def last_of(own, before):
        own = jnp.where(own[None, :] <= positions[:, None], own[None, :], -rows)
        return jnp.maximum(jnp.max(own, axis=1), before - rows)

    last_start = last_of(starts, prior)
    padded_last = jnp.concatenate([last_start, last_of(following, starts[-1])[:taps] + rows])[None]
    edge = jnp.zeros((groups, taps), jnp.float32)
    base_back = jnp.concatenate([taps32, edge], axis=1)
    base_fore = jnp.concatenate([edge[:, :1], taps32[:, ::-1], edge[:, 1:]], axis=1)
    (
        own_out, in_w, grad_half, grad_out, other_up, square_sum, padded_last, last_col, base_back, base_fore,
        columns,
    ) = fence(
        own_out, in_w, grad_half, grad_out, other_up, square_sum, padded_last, last_start[:, None], base_back,
        base_fore, columns,
    )

    ahead, behind = {0: in_w}, {0: in_w}
    ahead[1], behind[1] = both_ways(in_w, in_w)
    sib_out = sibling(own_out)
    other_down = lax.ppermute(grad_out[spans[1]], ("x", "c"), CYCLE)
    grad_other = jnp.concatenate([other_up, other_down], axis=0)
    k_recv, q_recv = exchanged(keys), [exchanged(queries[spans[0]])]
    if n_chan > 1:
        grad_half = lax.all_gather(grad_half, "h", axis=1, tiled=True)
        grad_other = lax.all_gather(grad_other, "h", axis=1, tiled=True)
    grads = jnp.concatenate([grad_half, grad_other], axis=1)
    mix_grad = mix_matmul(columns, grads, own_out, sib_out)
    ahead[1], behind[1], mix_grad, k_recv, keys, q_recv[0], queries = fence(
        ahead[1], behind[1], mix_grad, k_recv, keys, q_recv[0], queries
    )

    ahead[2], behind[2] = both_ways(ahead[1], behind[1])
    q_recv.append(exchanged(queries[spans[1]]))
    q_recv[1], queries, values, mix_grad = fence(q_recv[1], queries, values, mix_grad)
    middle = width // 2
    parts = (slice(0, middle), slice(middle, width))
    v_recv = [exchanged(values[:, part]) for part in parts]
    own_k = jnp.where(x == c, keys, k_recv)
    own_q = jnp.where(x == c, queries, jnp.concatenate(q_recv, axis=0))
    head = (mix_grad[:taps] * own_q[:taps].astype(jnp.float32)).astype(jnp.bfloat16)
    head = lax.ppermute(head, ("o", "c"), backward)
    conv, v_grad = conv_call(
        backward_kernel, "backward_conv", base_back, padded_last, None,
        [own_k, own_q, mix_grad], [jnp.float32, jnp.bfloat16], taps, per, width,
    )
    conv, v_grad = ending_call(
        base_back, padded_last, head, [own_k, own_q, mix_grad], conv, v_grad, taps, per
    )
    *v_recv, values, conv, v_grad = fence(*v_recv, values, conv, v_grad)

    def forward(at):
        own_v = jnp.where(x == c, values[:, parts[at]], v_recv[at])
        return conv_call(
            forward_kernel, "forward_conv", base_fore, last_col, tail,
            [own_k, own_v, mix_grad, conv], [jnp.bfloat16, jnp.bfloat16], taps, per, middle, at * middle,
        )

    q_left, k_left = forward(0)
    sib_q, sib_k, sib_v = sibling(q_left), sibling(k_left), sibling(v_grad)
    ahead[2], behind[2], q_left, k_left, v_grad, sib_q, sib_k, sib_v, v_recv[1] = fence(
        ahead[2], behind[2], q_left, k_left, v_grad, sib_q, sib_k, sib_v, v_recv[1]
    )

    ahead[3], behind[3] = both_ways(ahead[2], behind[2])
    q_right, k_right = forward(1)
    own_grads = [[q_left, q_right], [k_left, k_right], [v_grad]]
    sib_grads = [[sib_q, sibling(q_right)], [sib_k, sibling(k_right)], [sib_v]]

    def partial_sums(weights):
        ours, theirs = project(own_grads, sib_grads, weights)
        return jnp.where(c == x, ours, theirs), jnp.where(c == x, theirs, ours)

    def summed(keep, received):
        return (keep.astype(jnp.float32) + received.astype(jnp.float32)).astype(jnp.bfloat16)

    def over_x(block):
        return lax.ppermute(block, "x", PAIR)

    norms = []
    ready = [ahead[2], behind[2]]
    for s in range(3, far + 1):
        if 3 < s < far:
            ahead[s], behind[s] = both_ways(ahead[s - 1], behind[s - 1])
        elif s == far:
            up, down = far_halves(ahead[s - 1], behind[s - 1], 1)
        early = partial_sums([in_w, ahead[1], behind[1]]) if s == 3 else None
        keep, send = partial_sums(ready)
        if early:
            first, received = early[0], over_x(early[1])
            ahead[s], behind[s], first, received, keep, send = fence(
                ahead[s], behind[s], first, received, keep, send
            )
            norms.append(summed(first, received))
            ready = [ahead[s], behind[s]]
        elif s < far:
            ahead[s], behind[s], keep, send = fence(ahead[s], behind[s], keep, send)
            ready = [ahead[s], behind[s]]
        else:
            up, down, keep, send = fence(up, down, keep, send)
            ready = [jnp.concatenate([up, down], axis=1)]
        norms.append(summed(keep, over_x(send)))
    keep, send = partial_sums(ready)
    norms.append(summed(keep, over_x(send)))
    if n_chan > 1:
        norm = jnp.concatenate(norms, axis=0)
        slot = jnp.zeros((count,), jnp.int32).at[sources].set(jnp.arange(count, dtype=jnp.int32))
        norm = lax.psum_scatter(
            jnp.take(norm, slot, axis=0), "h", scatter_dimension=0, tiled=True
        )
        other = lax.ppermute(norm, "c", PAIR)
        slot = jnp.arange(count, dtype=jnp.int32) - h * (count // n_chan)
    else:
        norm = jnp.concatenate(norms, axis=0)
        other = jnp.concatenate([lax.ppermute(n, "c", PAIR) for n in norms], axis=0)
        slot = jnp.zeros((count,), jnp.int32).at[sources].set(jnp.arange(count, dtype=jnp.int32))
    mine = (h * 2 + c) * wide + jnp.arange(wide, dtype=jnp.int32)
    slots = slot[mine // 2]
    at = jnp.stack([slots, slots, (mine % 2 == c).astype(jnp.int32)])
    norm_grad, cross = pick(at, norm, other, block_input, norm_gain[None])
    cross_sum, square_sum = lax.psum((cross, square_sum), ("h", "c"))
    inverse = lax.rsqrt(square_sum / features + EPSILON)
    scaled = norm_gain.astype(jnp.float32)[None, :] * norm_grad.astype(jnp.float32)
    result = (
        grad_out.astype(jnp.float32)
        + inverse * scaled
        - source_in * (inverse * inverse * inverse) * cross_sum / features
    )
    return result.astype(jnp.bfloat16)


def solution(mesh):
    outer, n_chan = mesh.shape["ctx"] // 2, mesh.shape["ch"] // 2
    split = Mesh(mesh.devices.reshape(outer, 2, n_chan, 2), ("o", "x", "h", "c"))
    ring = list(range(0, outer, 2)) + list(range(outer - 1, 0, -2))
    tok, chan = ("o", "x"), ("h", "c")
    placed = (
        P(tok, chan),
        P(tok, chan),
        P(chan),
        P(tok, chan),
        P(tok, chan),
        P(tok, chan),
        P(chan, None),
        P(tok, None),
        P(tok, None, chan),
        P(chan, tok),
    )
    return jax.shard_map(
        functools.partial(on_device, ring, n_chan),
        mesh=split,
        in_specs=placed,
        out_specs=P(tok, chan),
        check_vma=False,
    )
```

```python
import functools

import jax
import jax.numpy as jnp
from jax import lax
from jax.experimental import pallas as pl
from jax.experimental.pallas import tpu as pltpu
from jax.sharding import Mesh
from jax.sharding import PartitionSpec as P

LANES = 128
EPSILON = 1e-05
VMEM_BYTES = 52 * 1024 * 1024

BRIEF = pl.CostEstimate(flops=1024, bytes_accessed=1024, transcendentals=0)

SWAP = [(1, 2), (2, 1)]
CYCLE = [(0, 2), (1, 0), (2, 3), (3, 1)]
PAIR = [(0, 1), (1, 0)]


def fence(*blocks):
    return lax.optimization_barrier(blocks)


def params(parallel):
    return pltpu.CompilerParams(
        dimension_semantics=("arbitrary",) * parallel, vmem_limit_bytes=VMEM_BYTES
    )


def toeplitz_into(table_ref, base_ref, taps, count):
    for q in range(count):
        row = jnp.broadcast_to(base_ref[q : q + 1, :], (taps, 2 * taps))
        band = pltpu.roll(row, 0, 1, stride=1, stride_axis=0)
        table_ref[q * taps : (q + 1) * taps, :] = band.astype(table_ref.dtype)


def banded(table, keep, source, taps, count):
    table = table.reshape(count, taps, 2 * taps)
    masked = (table * keep[None]).reshape(count * taps, 2 * taps)
    wide = jnp.dot(masked, source, preferred_element_type=jnp.float32)
    width = source.shape[1]
    owner = lax.broadcasted_iota(jnp.int32, (taps, width), 1) // (width // count)
    total = wide[:taps]
    for q in range(1, count):
        total = jnp.where(owner == q, wide[q * taps : (q + 1) * taps], total)
    return total


def forward_kernel(
    taps, count, base_ref, last_ref, tail_ref, keys_ref, values_ref, mix_ref, q_ref, table_ref, source_ref,
):
    rows, width = keys_ref.shape
    parts = width // LANES
    toeplitz_into(table_ref, base_ref, taps, parts * count)
    source_ref[:taps, :] = tail_ref[...]
    source_ref[taps:, :] = (keys_ref[...].astype(jnp.float32) * values_ref[...].astype(jnp.float32)).astype(
        jnp.bfloat16
    )

    def tile(i, carry):
        row = pl.multiple_of(i * taps, taps)
        col = lax.broadcasted_iota(jnp.int32, (taps, 2 * taps), 1) + (i - 1) * taps
        keep = jnp.where(col >= last_ref[pl.ds(row, taps), :], 1.0, 0.0).astype(jnp.bfloat16)
        for p in range(parts):
            lanes = slice(p * LANES, (p + 1) * LANES)
            table = table_ref[p * count * taps : (p + 1) * count * taps, :]
            mixed = banded(table, keep, source_ref[pl.ds(row, 2 * taps), lanes], taps, count)
            at = (pl.ds(row, taps), lanes)
            q_ref[at] = (mix_ref[at] * mixed).astype(q_ref.dtype)
        return carry

    lax.fori_loop(0, rows // taps, tile, 0)


def backward_kernel(
    taps, count, base_ref, last_ref, head_ref, keys_ref, values_ref, queries_ref, mix_ref,
    k_ref, v_ref, table_ref, source_ref,
):
    rows, width = keys_ref.shape
    parts = width // LANES
    toeplitz_into(table_ref, base_ref, taps, parts * count)
    source_ref[:rows, :] = (mix_ref[...] * queries_ref[...].astype(jnp.float32)).astype(jnp.bfloat16)
    source_ref[rows:, :] = head_ref[...]

    def tile(i, carry):
        row = pl.multiple_of(i * taps, taps)
        at_row = lax.broadcasted_iota(jnp.int32, (taps, 2 * taps), 0) + i * taps
        keep = jnp.where(at_row >= last_ref[:, pl.ds(row, 2 * taps)], 1.0, 0.0).astype(jnp.bfloat16)
        for p in range(parts):
            lanes = slice(p * LANES, (p + 1) * LANES)
            table = table_ref[p * count * taps : (p + 1) * count * taps, :]
            conv = banded(table, keep, source_ref[pl.ds(row, 2 * taps), lanes], taps, count)
            at = (pl.ds(row, taps), lanes)
            k_ref[at] = (conv * values_ref[at].astype(jnp.float32)).astype(k_ref.dtype)
            v_ref[at] = (conv * keys_ref[at].astype(jnp.float32)).astype(v_ref.dtype)
        return carry

    lax.fori_loop(0, rows // taps, tile, 0)


def conv_call(kernel, name, base, last, edge, operands, outs, taps, per, width, start=0):
    rows = operands[0].shape[0]
    cols = min(width, 4 * LANES)
    count = cols // LANES * per
    skip = start // cols
    slab = pl.BlockSpec((rows, cols), lambda g: (0, g + skip))
    return pl.pallas_call(
        functools.partial(kernel, taps, per),
        grid=(width // cols,),
        in_specs=[
            pl.BlockSpec((count, 2 * taps), lambda g: (g + skip, 0)),
            pl.BlockSpec(last.shape, lambda g: (0, 0)),
            pl.BlockSpec((taps, cols), lambda g: (0, g + skip)),
        ]
        + [slab] * len(operands),
        out_specs=[pl.BlockSpec((rows, cols), lambda g: (0, g))] * outs,
        out_shape=[jax.ShapeDtypeStruct((rows, width), jnp.bfloat16)] * outs,
        scratch_shapes=[
            pltpu.VMEM((count * taps, 2 * taps), jnp.bfloat16),
            pltpu.VMEM((rows + taps, cols), jnp.bfloat16),
        ],
        compiler_params=params(1),
        cost_estimate=BRIEF,
        name=name,
    )(base, last, edge, *operands)


NT = (((1,), (1,)), ((), ()))


def mix_kernel(at_ref, *refs):
    lefts, own_ref, sib_ref, out_ref = refs[:-3], *refs[-3:]
    step = pl.program_id(1)
    both = None
    for n, left in enumerate(lefts):
        right = (own_ref, sib_ref)[n % 2][n // 2]
        part = lax.dot_general(left[...], right, NT, preferred_element_type=jnp.float32)
        both = part if both is None else both + part

    @pl.when(step == 0)
    def _():
        out_ref[...] = both

    @pl.when(step > 0)
    def _():
        out_ref[...] += both


def mix_matmul(at, grads, own, sib):
    rows = grads.shape[0]
    blocks, width, feats = own.shape
    cols = min(width, 1024)
    lefts = [
        pl.BlockSpec((rows, feats), lambda n, j, at, side=side, k=k: (0, at[side, 2 * j + k]))
        for k in range(2)
        for side in range(2)
    ]
    right = pl.BlockSpec((2, cols, feats), lambda n, j, at: (j, n, 0))
    return pl.pallas_call(
        mix_kernel,
        grid_spec=pltpu.PrefetchScalarGridSpec(
            num_scalar_prefetch=1,
            grid=(width // cols, blocks // 2),
            in_specs=lefts + [right, right],
            out_specs=pl.BlockSpec((rows, cols), lambda n, j, at: (0, n)),
        ),
        out_shape=jax.ShapeDtypeStruct((rows, width), jnp.float32),
        compiler_params=params(2),
        cost_estimate=BRIEF,
        name="mix_matmul",
    )(at, *[grads] * len(lefts), own, sib)


def project_kernel(places, blocks, *refs):
    half = pl.num_programs(0) // 2
    own, sib = refs[: len(places)], refs[len(places) : 2 * len(places)]
    weights, outs = refs[2 * len(places) : -2], refs[-2:]

    def into(grads, out_ref):
        for n in range(blocks):
            total = None
            for grad, (b, left) in zip(grads, places):
                right = weights[n][b, :, left : left + grad.shape[1]]
                part = lax.dot_general(grad[...], right, NT, preferred_element_type=jnp.float32)
                total = part if total is None else total + part
            out_ref[n] = total.astype(out_ref.dtype)

    @pl.when(pl.program_id(0) < half)
    def _():
        into(own, outs[0])

    @pl.when(pl.program_id(0) >= half)
    def _():
        into(sib, outs[1])


def project(own, sib, weights):
    blocks = len(weights)
    branches, feats, width = weights[0].shape
    rows = own[0][0].shape[0]
    places = [
        (b, sum(p.shape[1] for p in pieces[:at])) for b, pieces in enumerate(own) for at in range(len(pieces))
    ]
    own, sib = [p for pieces in own for p in pieces], [p for pieces in sib for p in pieces]
    half = 2
    step = rows // half

    def first(i):
        return jnp.minimum(i, half - 1)

    def second(i):
        return jnp.maximum(i - half, 0)

    out = jax.ShapeDtypeStruct((blocks, rows, feats), jnp.bfloat16)
    return pl.pallas_call(
        functools.partial(project_kernel, places, blocks),
        grid=(2 * half,),
        in_specs=[pl.BlockSpec((step, p.shape[1]), lambda i: (first(i), 0)) for p in own]
        + [pl.BlockSpec((step, p.shape[1]), lambda i: (second(i), 0)) for p in sib]
        + [
            pl.BlockSpec((branches, feats, width), lambda i: (0, 0, 0), pipeline_mode=pl.Buffered(1))
        ]
        * blocks,
        out_specs=[
            pl.BlockSpec((blocks, step, feats), lambda i: (0, first(i), 0)),
            pl.BlockSpec((blocks, step, feats), lambda i: (0, second(i), 0)),
        ],
        out_shape=[out, out],
        compiler_params=params(1),
        cost_estimate=BRIEF,
        name="project",
    )(*own, *sib, *weights)


def pick_kernel(at_ref, own_ref, sib_ref, input_ref, gain_ref, norm_ref, cross_ref):
    step = pl.program_id(0)
    ours = (lax.broadcasted_iota(jnp.int32, own_ref.shape[1:], 0) * 0 + at_ref[2, step]) == 1
    norm = jnp.where(ours, own_ref[0].astype(jnp.float32), sib_ref[0].astype(jnp.float32))
    norm_ref[...] = norm.astype(norm_ref.dtype)
    part = jnp.sum(
        gain_ref[...].astype(jnp.float32) * norm * input_ref[...].astype(jnp.float32),
        axis=1,
        keepdims=True,
    )

    @pl.when(step == 0)
    def _():
        cross_ref[...] = part

    @pl.when(step > 0)
    def _():
        cross_ref[...] += part


def pick(at, own, sib, block_input, gain):
    rows, width = block_input.shape
    feats = own.shape[2]
    return pl.pallas_call(
        pick_kernel,
        grid_spec=pltpu.PrefetchScalarGridSpec(
            num_scalar_prefetch=1,
            grid=(width // feats,),
            in_specs=[
                pl.BlockSpec((1, rows, feats), lambda j, at: (at[0, j], 0, 0)),
                pl.BlockSpec((1, rows, feats), lambda j, at: (at[1, j], 0, 0)),
                pl.BlockSpec((rows, feats), lambda j, at: (0, j)),
                pl.BlockSpec((1, feats), lambda j, at: (0, j)),
            ],
            out_specs=[
                pl.BlockSpec((rows, feats), lambda j, at: (0, j)),
                pl.BlockSpec((rows, 1), lambda j, at: (0, 0)),
            ],
        ),
        out_shape=[
            jax.ShapeDtypeStruct((rows, width), jnp.bfloat16),
            jax.ShapeDtypeStruct((rows, 1), jnp.float32),
        ],
        compiler_params=params(1),
        cost_estimate=BRIEF,
        name="pick",
    )(at, own, sib, block_input, gain)


def on_device(
    ring,
    n_chan,
    grad_out,
    block_input,
    norm_gain,
    queries,
    keys,
    values,
    filters,
    doc_starts,
    in_weight,
    out_weight,
):
    rows, width = grad_out.shape
    groups, taps = filters.shape
    feats, branches = in_weight.shape[:2]
    count = len(ring)
    per = LANES * groups // width
    features = feats * 2 * count
    o, x, h, c = (lax.axis_index(a) for a in ("o", "x", "h", "c"))
    order = jnp.array(ring, jnp.int32)
    place = jnp.array([ring.index(i) for i in range(count)], jnp.int32)
    position = place[o]
    far = count // 2
    forth = [(ring[i], ring[(i + 1) % count]) for i in range(count)]
    back = [(b, a) for a, b in forth]

    def exchanged(block):
        return lax.ppermute(block, ("x", "c"), SWAP)

    def swapped(block):
        return jnp.where(x == c, block, exchanged(block))

    def sibling(block):
        return lax.ppermute(block, "c", PAIR)

    def both_ways(up, down):
        return lax.ppermute(up, ("o",), forth), lax.ppermute(down, ("o",), back)

    def far_halves(up, down, axis):
        half = up.shape[axis] // 2
        return both_ways(
            lax.slice_in_dim(up, 0, half, axis=axis),
            lax.slice_in_dim(down, half, 2 * half, axis=axis),
        )

    def neighbour(block, distance):
        route = []
        for i in range(count):
            for core in range(2):
                source = i * 2 + core + distance
                if 0 <= source < 2 * count:
                    route += [(source * 2 + side, (i * 2 + side) * 2 + core) for side in range(2)]
        return lax.ppermute(block, ("o", "x", "c"), route)

    starts = swapped(doc_starts)[0]
    prior = neighbour(doc_starts, -1)[0, -1]
    following = neighbour(doc_starts, 1)[0]
    tail = (keys[rows - taps :].astype(jnp.float32) * values[rows - taps :].astype(jnp.float32)).astype(
        jnp.bfloat16
    )
    taps32 = swapped(filters).astype(jnp.float32)
    out_w = swapped(out_weight)
    in_w = jnp.swapaxes(in_weight, 0, 1)
    out_w, in_w, grad_out, taps32, starts, prior, following, tail = fence(
        out_w, in_w, grad_out, taps32, starts, prior, following, tail
    )

    in_recv = exchanged(in_w)
    blocks = [out_w]
    up = down = out_w
    for s in range(1, far):
        up, down = both_ways(up, down)
        if s == far - 2:
            up, down, in_recv, in_w, grad_out, queries = fence(up, down, in_recv, in_w, grad_out, queries)
        blocks += [up, down]
    in_w = jnp.where(x == c, in_w, in_recv)
    half_recv = exchanged(grad_out)
    first_q = exchanged(queries[:taps])
    blocks.append(jnp.concatenate(far_halves(up, down, 0), axis=0))
    own_out = jnp.stack(blocks)
    source_in = block_input.astype(jnp.float32)
    square_sum = jnp.sum(source_in * source_in, axis=1, keepdims=True)
    distances = [0] + [d for s in range(1, far) for d in (-s, s)] + [far]
    sources = order[(position + jnp.array(distances, jnp.int32)) % count]
    wide = width // feats

    def column(parity):
        block = sources * 2 + parity
        owner = block // wide
        side = jnp.where(owner % 2 == x, 0, 1)
        return side * (n_chan * wide) + (owner // 2) * wide + block % wide

    columns = jnp.stack([column(c), column(1 - c)])
    slabs = 2 * count
    backward = [(i + 1, i) for i in range(slabs - 1)]
    positions = jnp.arange(rows, dtype=jnp.int32)

    def last_of(own, before):
        own = jnp.where(own[None, :] <= positions[:, None], own[None, :], -rows)
        return jnp.maximum(jnp.max(own, axis=1), before - rows)

    last_start = last_of(starts, prior)
    padded_last = jnp.concatenate([last_start, last_of(following, starts[-1])[:taps] + rows])[None]
    edge = jnp.zeros((groups, taps), jnp.float32)
    base_back = jnp.concatenate([taps32, edge], axis=1)
    base_fore = jnp.concatenate([edge[:, :1], taps32[:, ::-1], edge[:, 1:]], axis=1)
    (
        own_out, in_w, half_recv, first_q, grad_out, queries, square_sum, padded_last, last_col, base_back,
        base_fore, columns,
    ) = fence(
        own_out, in_w, half_recv, first_q, grad_out, queries, square_sum, padded_last, last_start[:, None],
        base_back, base_fore, columns,
    )

    ahead, behind = {0: in_w}, {0: in_w}
    ahead[1], behind[1] = both_ways(in_w, in_w)
    sib_out = sibling(own_out)
    grad_other = lax.ppermute(grad_out, ("x", "c"), CYCLE)
    grad_other, keys, tail = fence(grad_other, keys, tail)
    k_recv = exchanged(keys)
    tail = neighbour(tail, -1)
    grad_half = jnp.where(x == c, grad_out, half_recv)
    if n_chan > 1:
        grad_half = lax.all_gather(grad_half, "h", axis=1, tiled=True)
        grad_other = lax.all_gather(grad_other, "h", axis=1, tiled=True)
    grads = jnp.concatenate([grad_half, grad_other], axis=1)
    mix_grad = mix_matmul(columns, grads, own_out, sib_out)
    ahead[1], behind[1], mix_grad, k_recv, keys, tail, values = fence(
        ahead[1], behind[1], mix_grad, k_recv, keys, tail, values
    )

    ahead[2], behind[2] = both_ways(ahead[1], behind[1])
    v_recv = exchanged(values)
    head = mix_grad[:taps] * jnp.where(x == c, queries[:taps], first_q).astype(jnp.float32)
    head = lax.ppermute(head.astype(jnp.bfloat16), ("o", "c"), backward)
    own_k = jnp.where(x == c, keys, k_recv)
    v_recv, values, own_k, queries = fence(v_recv, values, own_k, queries)
    q_recv = exchanged(queries)
    own_v = jnp.where(x == c, values, v_recv)
    middle = width // 2

    def halves(kernel, name, *operands, outs):
        return [
            conv_call(kernel, name, *operands, outs, taps, per, middle, start) for start in (0, middle)
        ]

    (q_left,), (q_right,) = halves(
        forward_kernel, "forward_conv", base_fore, last_col, tail, [own_k, own_v, mix_grad], outs=1
    )
    sib_left = sibling(q_left)
    ahead[2], behind[2], q_left, q_right, sib_left, head, q_recv, queries = fence(
        ahead[2], behind[2], q_left, q_right, sib_left, head, q_recv, queries
    )

    ahead[3], behind[3] = both_ways(ahead[2], behind[2])
    own_q = jnp.where(x == c, queries, q_recv)
    grads = halves(
        backward_kernel, "backward_conv", base_back, padded_last, head, [own_k, own_v, own_q, mix_grad], outs=2
    )
    own_grads = [[q_left, q_right]] + [[half[b] for half in grads] for b in range(2)]
    sib_grads = [[sib_left, sibling(q_right)]] + [[sibling(half[b]) for half in grads] for b in range(2)]

    def partial_sums(weights):
        ours, theirs = project(own_grads, sib_grads, weights)
        return jnp.where(c == x, ours, theirs), jnp.where(c == x, theirs, ours)

    def summed(keep, received):
        return (keep.astype(jnp.float32) + received.astype(jnp.float32)).astype(jnp.bfloat16)

    def over_x(block):
        return lax.ppermute(block, "x", PAIR)

    norms = []
    ready = [ahead[2], behind[2]]
    for s in range(3, far + 1):
        if 3 < s < far:
            ahead[s], behind[s] = both_ways(ahead[s - 1], behind[s - 1])
        elif s == far:
            up, down = far_halves(ahead[s - 1], behind[s - 1], 1)
        early = partial_sums([in_w, ahead[1], behind[1]]) if s == 3 else None
        keep, send = partial_sums(ready)
        if early:
            first, received = early[0], over_x(early[1])
            ahead[s], behind[s], first, received, keep, send = fence(
                ahead[s], behind[s], first, received, keep, send
            )
            norms.append(summed(first, received))
            ready = [ahead[s], behind[s]]
        elif s < far:
            ahead[s], behind[s], keep, send = fence(ahead[s], behind[s], keep, send)
            ready = [ahead[s], behind[s]]
        else:
            up, down, keep, send = fence(up, down, keep, send)
            ready = [jnp.concatenate([up, down], axis=1)]
        norms.append(summed(keep, over_x(send)))
    keep, send = partial_sums(ready)
    norms.append(summed(keep, over_x(send)))
    if n_chan > 1:
        norm = jnp.concatenate(norms, axis=0)
        slot = jnp.zeros((count,), jnp.int32).at[sources].set(jnp.arange(count, dtype=jnp.int32))
        norm = lax.psum_scatter(
            jnp.take(norm, slot, axis=0), "h", scatter_dimension=0, tiled=True
        )
        other = lax.ppermute(norm, "c", PAIR)
        slot = jnp.arange(count, dtype=jnp.int32) - h * (count // n_chan)
    else:
        norm = jnp.concatenate(norms, axis=0)
        other = jnp.concatenate([lax.ppermute(n, "c", PAIR) for n in norms], axis=0)
        slot = jnp.zeros((count,), jnp.int32).at[sources].set(jnp.arange(count, dtype=jnp.int32))
    mine = (h * 2 + c) * wide + jnp.arange(wide, dtype=jnp.int32)
    slots = slot[mine // 2]
    at = jnp.stack([slots, slots, (mine % 2 == c).astype(jnp.int32)])
    norm_grad, cross = pick(at, norm, other, block_input, norm_gain[None])
    cross_sum, square_sum = lax.psum((cross, square_sum), ("h", "c"))
    inverse = lax.rsqrt(square_sum / features + EPSILON)
    scaled = norm_gain.astype(jnp.float32)[None, :] * norm_grad.astype(jnp.float32)
    result = (
        grad_out.astype(jnp.float32)
        + inverse * scaled
        - source_in * (inverse * inverse * inverse) * cross_sum / features
    )
    return result.astype(jnp.bfloat16)


def solution(mesh):
    outer, n_chan = mesh.shape["ctx"] // 2, mesh.shape["ch"] // 2
    split = Mesh(mesh.devices.reshape(outer, 2, n_chan, 2), ("o", "x", "h", "c"))
    ring = list(range(0, outer, 2)) + list(range(outer - 1, 0, -2))
    tok, chan = ("o", "x"), ("h", "c")
    placed = (
        P(tok, chan),
        P(tok, chan),
        P(chan),
        P(tok, chan),
        P(tok, chan),
        P(tok, chan),
        P(chan, None),
        P(tok, None),
        P(tok, None, chan),
        P(chan, tok),
    )
    return jax.shard_map(
        functools.partial(on_device, ring, n_chan),
        mesh=split,
        in_specs=placed,
        out_specs=P(tok, chan),
        check_vma=False,
    )
```

```python
import functools

import jax
import jax.numpy as jnp
from jax import lax
from jax.experimental import pallas as pl
from jax.experimental.pallas import tpu as pltpu
from jax.sharding import Mesh
from jax.sharding import PartitionSpec as P

LANES = 128
EPSILON = 1e-05
VMEM_BYTES = 52 * 1024 * 1024

BRIEF = pl.CostEstimate(flops=1024, bytes_accessed=1024, transcendentals=0)

SWAP = [(1, 2), (2, 1)]
CYCLE = [(0, 2), (1, 0), (2, 3), (3, 1)]
PAIR = [(0, 1), (1, 0)]


def fence(*blocks):
    return lax.optimization_barrier(blocks)


def params(parallel):
    return pltpu.CompilerParams(
        dimension_semantics=("arbitrary",) * parallel, vmem_limit_bytes=VMEM_BYTES
    )


def toeplitz_into(table_ref, base_ref, taps, count):
    for q in range(count):
        row = jnp.broadcast_to(base_ref[q : q + 1, :], (taps, 2 * taps))
        band = pltpu.roll(row, 0, 1, stride=1, stride_axis=0)
        table_ref[q * taps : (q + 1) * taps, :] = band.astype(table_ref.dtype)


def banded(table, keep, source, taps, count):
    table = table.reshape(count, taps, 2 * taps)
    masked = (table * keep[None]).reshape(count * taps, 2 * taps)
    wide = jnp.dot(masked, source, preferred_element_type=jnp.float32)
    width = source.shape[1]
    owner = lax.broadcasted_iota(jnp.int32, (taps, width), 1) // (width // count)
    total = wide[:taps]
    for q in range(1, count):
        total = jnp.where(owner == q, wide[q * taps : (q + 1) * taps], total)
    return total


def forward_kernel(
    taps, count, base_ref, last_ref, tail_ref, keys_ref, values_ref, mix_ref, q_ref, table_ref, source_ref,
):
    rows, width = keys_ref.shape
    parts = width // LANES
    toeplitz_into(table_ref, base_ref, taps, parts * count)
    source_ref[:taps, :] = tail_ref[...]
    source_ref[taps:, :] = (keys_ref[...].astype(jnp.float32) * values_ref[...].astype(jnp.float32)).astype(
        jnp.bfloat16
    )

    def tile(i, carry):
        row = pl.multiple_of(i * taps, taps)
        col = lax.broadcasted_iota(jnp.int32, (taps, 2 * taps), 1) + (i - 1) * taps
        keep = jnp.where(col >= last_ref[pl.ds(row, taps), :], 1.0, 0.0).astype(jnp.bfloat16)
        for p in range(parts):
            lanes = slice(p * LANES, (p + 1) * LANES)
            table = table_ref[p * count * taps : (p + 1) * count * taps, :]
            mixed = banded(table, keep, source_ref[pl.ds(row, 2 * taps), lanes], taps, count)
            at = (pl.ds(row, taps), lanes)
            q_ref[at] = (mix_ref[at] * mixed).astype(q_ref.dtype)
        return carry

    lax.fori_loop(0, rows // taps, tile, 0)


def backward_kernel(
    taps, count, base_ref, last_ref, head_ref, keys_ref, values_ref, queries_ref, mix_ref,
    k_ref, v_ref, table_ref, source_ref,
):
    rows, width = keys_ref.shape
    parts = width // LANES
    toeplitz_into(table_ref, base_ref, taps, parts * count)
    source_ref[:rows, :] = (mix_ref[...] * queries_ref[...].astype(jnp.float32)).astype(jnp.bfloat16)
    source_ref[rows:, :] = head_ref[...]

    def tile(i, carry):
        row = pl.multiple_of(i * taps, taps)
        at_row = lax.broadcasted_iota(jnp.int32, (taps, 2 * taps), 0) + i * taps
        keep = jnp.where(at_row >= last_ref[:, pl.ds(row, 2 * taps)], 1.0, 0.0).astype(jnp.bfloat16)
        for p in range(parts):
            lanes = slice(p * LANES, (p + 1) * LANES)
            table = table_ref[p * count * taps : (p + 1) * count * taps, :]
            conv = banded(table, keep, source_ref[pl.ds(row, 2 * taps), lanes], taps, count)
            at = (pl.ds(row, taps), lanes)
            k_ref[at] = (conv * values_ref[at].astype(jnp.float32)).astype(k_ref.dtype)
            v_ref[at] = (conv * keys_ref[at].astype(jnp.float32)).astype(v_ref.dtype)
        return carry

    lax.fori_loop(0, rows // taps, tile, 0)


def conv_call(kernel, name, base, last, edge, operands, outs, taps, per, width, start=0):
    rows = operands[0].shape[0]
    cols = min(width, 4 * LANES)
    count = cols // LANES * per
    skip = start // cols
    slab = pl.BlockSpec((rows, cols), lambda g: (0, g + skip))
    return pl.pallas_call(
        functools.partial(kernel, taps, per),
        grid=(width // cols,),
        in_specs=[
            pl.BlockSpec((count, 2 * taps), lambda g: (g + skip, 0)),
            pl.BlockSpec(last.shape, lambda g: (0, 0)),
            pl.BlockSpec((taps, cols), lambda g: (0, g + skip)),
        ]
        + [slab] * len(operands),
        out_specs=[pl.BlockSpec((rows, cols), lambda g: (0, g))] * outs,
        out_shape=[jax.ShapeDtypeStruct((rows, width), jnp.bfloat16)] * outs,
        scratch_shapes=[
            pltpu.VMEM((count * taps, 2 * taps), jnp.bfloat16),
            pltpu.VMEM((rows + taps, cols), jnp.bfloat16),
        ],
        compiler_params=params(1),
        cost_estimate=BRIEF,
        name=name,
    )(base, last, edge, *operands)


NT = (((1,), (1,)), ((), ()))


def mix_kernel(at_ref, *refs):
    lefts, own_ref, sib_ref, out_ref = refs[:-3], *refs[-3:]
    step = pl.program_id(1)
    both = None
    for n, left in enumerate(lefts):
        right = (own_ref, sib_ref)[n % 2][n // 2]
        part = lax.dot_general(left[...], right, NT, preferred_element_type=jnp.float32)
        both = part if both is None else both + part

    @pl.when(step == 0)
    def _():
        out_ref[...] = both

    @pl.when(step > 0)
    def _():
        out_ref[...] += both


def mix_matmul(at, grads, own, sib):
    rows = grads.shape[0]
    blocks, width, feats = own.shape
    cols = min(width, 1024)
    lefts = [
        pl.BlockSpec((rows, feats), lambda n, j, at, side=side, k=k: (0, at[side, 2 * j + k]))
        for k in range(2)
        for side in range(2)
    ]
    right = pl.BlockSpec((2, cols, feats), lambda n, j, at: (j, n, 0))
    return pl.pallas_call(
        mix_kernel,
        grid_spec=pltpu.PrefetchScalarGridSpec(
            num_scalar_prefetch=1,
            grid=(width // cols, blocks // 2),
            in_specs=lefts + [right, right],
            out_specs=pl.BlockSpec((rows, cols), lambda n, j, at: (0, n)),
        ),
        out_shape=jax.ShapeDtypeStruct((rows, width), jnp.float32),
        compiler_params=params(2),
        cost_estimate=BRIEF,
        name="mix_matmul",
    )(at, *[grads] * len(lefts), own, sib)


def project_kernel(places, blocks, *refs):
    half = pl.num_programs(0) // 2
    own, sib = refs[: len(places)], refs[len(places) : 2 * len(places)]
    weights, outs = refs[2 * len(places) : -2], refs[-2:]

    def into(grads, out_ref):
        for n in range(blocks):
            total = None
            for grad, (b, left) in zip(grads, places):
                right = weights[n][b, :, left : left + grad.shape[1]]
                part = lax.dot_general(grad[...], right, NT, preferred_element_type=jnp.float32)
                total = part if total is None else total + part
            out_ref[n] = total.astype(out_ref.dtype)

    @pl.when(pl.program_id(0) < half)
    def _():
        into(own, outs[0])

    @pl.when(pl.program_id(0) >= half)
    def _():
        into(sib, outs[1])


def project(own, sib, weights):
    blocks = len(weights)
    branches, feats, width = weights[0].shape
    rows = own[0][0].shape[0]
    places = [
        (b, sum(p.shape[1] for p in pieces[:at])) for b, pieces in enumerate(own) for at in range(len(pieces))
    ]
    own, sib = [p for pieces in own for p in pieces], [p for pieces in sib for p in pieces]
    half = 2
    step = rows // half

    def first(i):
        return jnp.minimum(i, half - 1)

    def second(i):
        return jnp.maximum(i - half, 0)

    out = jax.ShapeDtypeStruct((blocks, rows, feats), jnp.bfloat16)
    return pl.pallas_call(
        functools.partial(project_kernel, places, blocks),
        grid=(2 * half,),
        in_specs=[pl.BlockSpec((step, p.shape[1]), lambda i: (first(i), 0)) for p in own]
        + [pl.BlockSpec((step, p.shape[1]), lambda i: (second(i), 0)) for p in sib]
        + [
            pl.BlockSpec((branches, feats, width), lambda i: (0, 0, 0), pipeline_mode=pl.Buffered(1))
        ]
        * blocks,
        out_specs=[
            pl.BlockSpec((blocks, step, feats), lambda i: (0, first(i), 0)),
            pl.BlockSpec((blocks, step, feats), lambda i: (0, second(i), 0)),
        ],
        out_shape=[out, out],
        compiler_params=params(1),
        cost_estimate=BRIEF,
        name="project",
    )(*own, *sib, *weights)


def pick_kernel(at_ref, own_ref, sib_ref, input_ref, gain_ref, norm_ref, cross_ref):
    step = pl.program_id(0)
    ours = (lax.broadcasted_iota(jnp.int32, own_ref.shape[1:], 0) * 0 + at_ref[2, step]) == 1
    norm = jnp.where(ours, own_ref[0].astype(jnp.float32), sib_ref[0].astype(jnp.float32))
    norm_ref[...] = norm.astype(norm_ref.dtype)
    part = jnp.sum(
        gain_ref[...].astype(jnp.float32) * norm * input_ref[...].astype(jnp.float32),
        axis=1,
        keepdims=True,
    )

    @pl.when(step == 0)
    def _():
        cross_ref[...] = part

    @pl.when(step > 0)
    def _():
        cross_ref[...] += part


def pick(at, own, sib, block_input, gain):
    rows, width = block_input.shape
    feats = own.shape[2]
    return pl.pallas_call(
        pick_kernel,
        grid_spec=pltpu.PrefetchScalarGridSpec(
            num_scalar_prefetch=1,
            grid=(width // feats,),
            in_specs=[
                pl.BlockSpec((1, rows, feats), lambda j, at: (at[0, j], 0, 0)),
                pl.BlockSpec((1, rows, feats), lambda j, at: (at[1, j], 0, 0)),
                pl.BlockSpec((rows, feats), lambda j, at: (0, j)),
                pl.BlockSpec((1, feats), lambda j, at: (0, j)),
            ],
            out_specs=[
                pl.BlockSpec((rows, feats), lambda j, at: (0, j)),
                pl.BlockSpec((rows, 1), lambda j, at: (0, 0)),
            ],
        ),
        out_shape=[
            jax.ShapeDtypeStruct((rows, width), jnp.bfloat16),
            jax.ShapeDtypeStruct((rows, 1), jnp.float32),
        ],
        compiler_params=params(1),
        cost_estimate=BRIEF,
        name="pick",
    )(at, own, sib, block_input, gain)


def finish_kernel(
    features, at_ref, own_ref, own_last_ref, sib_ref, sib_last_ref, input_ref, gain_ref, inverse_ref, grad_ref,
    out_ref, norm_ref,
):
    most = own_ref.shape[0]
    count, feats = most + 1, own_ref.shape[2]
    c = at_ref[2, 0]
    for parity, refs in ((c, (own_ref, own_last_ref)), (1 - c, (sib_ref, sib_last_ref))):
        norm_ref[parity, :most] = refs[0][...]
        norm_ref[parity, most:] = refs[1][...]

    cross = jnp.zeros(own_ref.shape[1:], jnp.float32)
    for n in range(count):
        for parity in range(2):
            block = at_ref[0, n] * 2 + parity
            left = pl.multiple_of(lax.rem(block, count) * feats, feats)
            half = lax.div(block, count)
            gain = gain_ref[half, :, pl.ds(left, feats)].astype(jnp.float32)
            source = input_ref[half, :, pl.ds(left, feats)].astype(jnp.float32)
            cross += gain * norm_ref[parity, n].astype(jnp.float32) * source
    inverse = inverse_ref[...]
    scale = inverse * inverse * inverse * jnp.sum(cross, axis=1, keepdims=True) / features
    for j in range(count):
        cols = slice(j * feats, (j + 1) * feats)
        block = c * count + j
        place = at_ref[1, lax.div(block, 2)]
        scaled = gain_ref[c, :, cols].astype(jnp.float32) * norm_ref[lax.rem(block, 2), place].astype(jnp.float32)
        result = grad_ref[:, cols].astype(jnp.float32) + inverse * scaled
        result -= input_ref[c, :, cols].astype(jnp.float32) * scale
        out_ref[:, cols] = result.astype(out_ref.dtype)


def finish(at, own, sib, inputs, gains, inverse, grad_out):
    rows, width = grad_out.shape
    most, _, feats = own[0].shape
    step = min(rows, 128)

    def some(blocks):
        return pl.BlockSpec((blocks, step, feats), lambda i, at: (0, i, 0))

    slab = pl.BlockSpec((step, width), lambda i, at: (i, 0))
    return pl.pallas_call(
        functools.partial(finish_kernel, 2 * width),
        grid_spec=pltpu.PrefetchScalarGridSpec(
            num_scalar_prefetch=1,
            grid=(rows // step,),
            in_specs=[
                some(most), some(1), some(most), some(1),
                pl.BlockSpec((2, step, width), lambda i, at: (0, i, 0)),
                pl.BlockSpec((2, 1, width), lambda i, at: (0, 0, 0)),
                pl.BlockSpec((step, 1), lambda i, at: (i, 0)),
                slab,
            ],
            out_specs=slab,
            scratch_shapes=[pltpu.VMEM((2, most + 1, step, feats), jnp.bfloat16)],
        ),
        out_shape=jax.ShapeDtypeStruct((rows, width), jnp.bfloat16),
        compiler_params=params(1),
        cost_estimate=BRIEF,
        name="finish",
    )(at, *own, *sib, inputs, gains, inverse, grad_out)


def on_device(
    ring,
    n_chan,
    grad_out,
    block_input,
    norm_gain,
    queries,
    keys,
    values,
    filters,
    doc_starts,
    in_weight,
    out_weight,
):
    rows, width = grad_out.shape
    groups, taps = filters.shape
    feats, branches = in_weight.shape[:2]
    count = len(ring)
    per = LANES * groups // width
    features = feats * 2 * count
    o, x, h, c = (lax.axis_index(a) for a in ("o", "x", "h", "c"))
    order = jnp.array(ring, jnp.int32)
    place = jnp.array([ring.index(i) for i in range(count)], jnp.int32)
    position = place[o]
    far = count // 2
    forth = [(ring[i], ring[(i + 1) % count]) for i in range(count)]
    back = [(b, a) for a, b in forth]

    def exchanged(block):
        return lax.ppermute(block, ("x", "c"), SWAP)

    def swapped(block):
        return jnp.where(x == c, block, exchanged(block))

    def sibling(block):
        return lax.ppermute(block, "c", PAIR)

    def both_ways(up, down):
        return lax.ppermute(up, ("o",), forth), lax.ppermute(down, ("o",), back)

    def far_halves(up, down, axis):
        half = up.shape[axis] // 2
        return both_ways(
            lax.slice_in_dim(up, 0, half, axis=axis),
            lax.slice_in_dim(down, half, 2 * half, axis=axis),
        )

    def neighbour(block, distance):
        route = []
        for i in range(count):
            for core in range(2):
                source = i * 2 + core + distance
                if 0 <= source < 2 * count:
                    route += [(source * 2 + side, (i * 2 + side) * 2 + core) for side in range(2)]
        return lax.ppermute(block, ("o", "x", "c"), route)

    starts = swapped(doc_starts)[0]
    prior = neighbour(doc_starts, -1)[0, -1]
    following = neighbour(doc_starts, 1)[0]
    tail = (keys[rows - taps :].astype(jnp.float32) * values[rows - taps :].astype(jnp.float32)).astype(
        jnp.bfloat16
    )
    taps32 = swapped(filters).astype(jnp.float32)
    out_w = swapped(out_weight)
    in_w = jnp.swapaxes(in_weight, 0, 1)
    out_w, in_w, grad_out, taps32, starts, prior, following, tail = fence(
        out_w, in_w, grad_out, taps32, starts, prior, following, tail
    )

    in_recv = exchanged(in_w)
    sib_in, sib_gain = sibling(block_input), sibling(norm_gain)
    blocks = [out_w]
    up = down = out_w
    for s in range(1, far):
        up, down = both_ways(up, down)
        if s == far - 2:
            up, down, in_recv, in_w, grad_out, queries, sib_in, sib_gain = fence(
                up, down, in_recv, in_w, grad_out, queries, sib_in, sib_gain
            )
        blocks += [up, down]
    in_w = jnp.where(x == c, in_w, in_recv)
    half_recv = exchanged(grad_out)
    first_q = exchanged(queries[:taps])
    blocks.append(jnp.concatenate(far_halves(up, down, 0), axis=0))
    own_out = jnp.stack(blocks)
    def in_order(own, sib):
        return jnp.where(c == 0, jnp.stack([own, sib]), jnp.stack([sib, own]))

    inputs, gains = in_order(block_input, sib_in), in_order(norm_gain, sib_gain)[:, None]
    square_sum = jnp.sum(jnp.square(inputs.astype(jnp.float32)), axis=(0, 2))[:, None]
    if n_chan > 1:
        square_sum = lax.psum(square_sum, "h")
    inverse = lax.rsqrt(square_sum / features + EPSILON)
    distances = [0] + [d for s in range(1, far) for d in (-s, s)] + [far]
    sources = order[(position + jnp.array(distances, jnp.int32)) % count]
    wide = width // feats

    def column(parity):
        block = sources * 2 + parity
        owner = block // wide
        side = jnp.where(owner % 2 == x, 0, 1)
        return side * (n_chan * wide) + (owner // 2) * wide + block % wide

    columns = jnp.stack([column(c), column(1 - c)])
    slabs = 2 * count
    backward = [(i + 1, i) for i in range(slabs - 1)]
    positions = jnp.arange(rows, dtype=jnp.int32)

    def last_of(own, before):
        own = jnp.where(own[None, :] <= positions[:, None], own[None, :], -rows)
        return jnp.maximum(jnp.max(own, axis=1), before - rows)

    last_start = last_of(starts, prior)
    padded_last = jnp.concatenate([last_start, last_of(following, starts[-1])[:taps] + rows])[None]
    edge = jnp.zeros((groups, taps), jnp.float32)
    base_back = jnp.concatenate([taps32, edge], axis=1)
    base_fore = jnp.concatenate([edge[:, :1], taps32[:, ::-1], edge[:, 1:]], axis=1)
    (
        own_out, in_w, half_recv, first_q, grad_out, queries, inverse, inputs, gains, padded_last, last_col,
        base_back, base_fore, columns,
    ) = fence(
        own_out, in_w, half_recv, first_q, grad_out, queries, inverse, inputs, gains, padded_last,
        last_start[:, None], base_back, base_fore, columns,
    )

    ahead, behind = {0: in_w}, {0: in_w}
    ahead[1], behind[1] = both_ways(in_w, in_w)
    sib_out = sibling(own_out)
    grad_other = lax.ppermute(grad_out, ("x", "c"), CYCLE)
    grad_other, keys, tail = fence(grad_other, keys, tail)
    k_recv = exchanged(keys)
    tail = neighbour(tail, -1)
    grad_half = jnp.where(x == c, grad_out, half_recv)
    if n_chan > 1:
        grad_half = lax.all_gather(grad_half, "h", axis=1, tiled=True)
        grad_other = lax.all_gather(grad_other, "h", axis=1, tiled=True)
    grads = jnp.concatenate([grad_half, grad_other], axis=1)
    mix_grad = mix_matmul(columns, grads, own_out, sib_out)
    ahead[1], behind[1], mix_grad, k_recv, keys, values = fence(
        ahead[1], behind[1], mix_grad, k_recv, keys, values
    )

    ahead[2], behind[2] = both_ways(ahead[1], behind[1])
    v_recv = exchanged(values)
    head = mix_grad[:taps] * jnp.where(x == c, queries[:taps], first_q).astype(jnp.float32)
    head = lax.ppermute(head.astype(jnp.bfloat16), ("o", "c"), backward)
    own_k = jnp.where(x == c, keys, k_recv)
    v_recv, values, own_k, queries, tail = fence(v_recv, values, own_k, queries, tail)
    q_recv = exchanged(queries)
    own_v = jnp.where(x == c, values, v_recv)
    middle = width // 2

    def halves(kernel, name, *operands, outs):
        return [
            conv_call(kernel, name, *operands, outs, taps, per, middle, start) for start in (0, middle)
        ]

    (q_left,), (q_right,) = halves(
        forward_kernel, "forward_conv", base_fore, last_col, tail, [own_k, own_v, mix_grad], outs=1
    )
    sib_left = sibling(q_left)
    ahead[2], behind[2], q_left, q_right, sib_left, head, q_recv, queries = fence(
        ahead[2], behind[2], q_left, q_right, sib_left, head, q_recv, queries
    )

    ahead[3], behind[3] = both_ways(ahead[2], behind[2])
    own_q = jnp.where(x == c, queries, q_recv)
    grads = halves(
        backward_kernel, "backward_conv", base_back, padded_last, head, [own_k, own_v, own_q, mix_grad], outs=2
    )
    own_grads = [[q_left, q_right]] + [[half[b] for half in grads] for b in range(2)]
    sib_grads = [[sib_left, sibling(q_right)]] + [[sibling(half[b]) for half in grads] for b in range(2)]

    def partial_sums(weights):
        ours, theirs = project(own_grads, sib_grads, weights)
        return jnp.where(c == x, ours, theirs), jnp.where(c == x, theirs, ours)

    def summed(keep, received):
        return (keep.astype(jnp.float32) + received.astype(jnp.float32)).astype(jnp.bfloat16)

    def over_x(block):
        return lax.ppermute(block, "x", PAIR)

    norms = []
    ready = [behind[1], ahead[2], behind[2]]
    for s in range(3, far + 1):
        if 3 < s < far:
            ahead[s], behind[s] = both_ways(ahead[s - 1], behind[s - 1])
        elif s == far:
            up, down = far_halves(ahead[s - 1], behind[s - 1], 1)
        early = partial_sums([in_w, ahead[1]]) if s == 3 else None
        keep, send = partial_sums(ready)
        if early:
            first, received = early[0], over_x(early[1])
            ahead[s], behind[s], first, received, keep, send = fence(
                ahead[s], behind[s], first, received, keep, send
            )
            norms.append(summed(first, received))
            ready = [ahead[s], behind[s]]
        elif s < far:
            ahead[s], behind[s], keep, send = fence(ahead[s], behind[s], keep, send)
            ready = [ahead[s], behind[s]]
        else:
            up, down, keep, send = fence(up, down, keep, send)
            ready = [jnp.concatenate([up, down], axis=1)]
        norms.append(summed(keep, over_x(send)))
    keep, send = partial_sums(ready)
    norms.append(summed(keep, over_x(send)))
    slot = jnp.zeros((count,), jnp.int32).at[sources].set(jnp.arange(count, dtype=jnp.int32))
    if n_chan == 1:
        others = [sibling(n) for n in norms]
        at = jnp.stack([sources, slot, jnp.full((count,), c, jnp.int32)])
        own, sib = (
            (jnp.concatenate(blocks[:-1], axis=0), blocks[-1]) for blocks in (norms, others)
        )
        return finish(at, own, sib, inputs, gains, inverse, grad_out)

    norm = lax.psum_scatter(
        jnp.take(jnp.concatenate(norms, axis=0), slot, axis=0), "h", scatter_dimension=0, tiled=True
    )
    other = sibling(norm)
    mine = (h * 2 + c) * wide + jnp.arange(wide, dtype=jnp.int32)
    slots = mine // 2 - h * (count // n_chan)
    at = jnp.stack([slots, slots, (mine % 2 == c).astype(jnp.int32)])
    norm_grad, cross = pick(at, norm, other, block_input, norm_gain[None])
    cross_sum = lax.psum(cross, ("h", "c"))
    scaled = norm_gain.astype(jnp.float32)[None, :] * norm_grad.astype(jnp.float32)
    result = (
        grad_out.astype(jnp.float32)
        + inverse * scaled
        - block_input.astype(jnp.float32) * (inverse * inverse * inverse) * cross_sum / features
    )
    return result.astype(jnp.bfloat16)


def solution(mesh):
    outer, n_chan = mesh.shape["ctx"] // 2, mesh.shape["ch"] // 2
    split = Mesh(mesh.devices.reshape(outer, 2, n_chan, 2), ("o", "x", "h", "c"))
    ring = list(range(0, outer, 2)) + list(range(outer - 1, 0, -2))
    tok, chan = ("o", "x"), ("h", "c")
    placed = (
        P(tok, chan),
        P(tok, chan),
        P(chan),
        P(tok, chan),
        P(tok, chan),
        P(tok, chan),
        P(chan, None),
        P(tok, None),
        P(tok, None, chan),
        P(chan, tok),
    )
    return jax.shard_map(
        functools.partial(on_device, ring, n_chan),
        mesh=split,
        in_specs=placed,
        out_specs=P(tok, chan),
        check_vma=False,
    )
```

```python
import functools

import jax
import jax.numpy as jnp
from jax import lax
from jax.experimental import pallas as pl
from jax.experimental.pallas import tpu as pltpu
from jax.sharding import Mesh
from jax.sharding import PartitionSpec as P

LANES = 128
EPSILON = 1e-05
VMEM_BYTES = 52 * 1024 * 1024

BRIEF = pl.CostEstimate(flops=1024, bytes_accessed=1024, transcendentals=0)

SWAP = [(1, 2), (2, 1)]
CYCLE = [(0, 2), (1, 0), (2, 3), (3, 1)]
PAIR = [(0, 1), (1, 0)]


def fence(*blocks):
    return lax.optimization_barrier(blocks)


def params(parallel):
    return pltpu.CompilerParams(
        dimension_semantics=("arbitrary",) * parallel, vmem_limit_bytes=VMEM_BYTES
    )


def toeplitz_into(table_ref, base_ref, taps, count):
    for q in range(count):
        row = jnp.broadcast_to(base_ref[q : q + 1, :], (taps, 2 * taps))
        band = pltpu.roll(row, 0, 1, stride=1, stride_axis=0)
        table_ref[q * taps : (q + 1) * taps, :] = band.astype(table_ref.dtype)


def banded(table, keep, source, taps, count):
    table = table.reshape(count, taps, 2 * taps)
    masked = (table * keep[None]).reshape(count * taps, 2 * taps)
    wide = jnp.dot(masked, source, preferred_element_type=jnp.float32)
    width = source.shape[1]
    owner = lax.broadcasted_iota(jnp.int32, (taps, width), 1) // (width // count)
    total = wide[:taps]
    for q in range(1, count):
        total = jnp.where(owner == q, wide[q * taps : (q + 1) * taps], total)
    return total


def forward_kernel(
    taps, count, base_ref, last_ref, tail_ref, keys_ref, values_ref, mix_ref, q_ref, table_ref, source_ref,
):
    rows, width = keys_ref.shape
    parts = width // LANES
    toeplitz_into(table_ref, base_ref, taps, parts * count)
    source_ref[:taps, :] = tail_ref[...]
    source_ref[taps:, :] = (keys_ref[...].astype(jnp.float32) * values_ref[...].astype(jnp.float32)).astype(
        jnp.bfloat16
    )

    def tile(i, carry):
        row = pl.multiple_of(i * taps, taps)
        col = lax.broadcasted_iota(jnp.int32, (taps, 2 * taps), 1) + (i - 1) * taps
        keep = jnp.where(col >= last_ref[pl.ds(row, taps), :], 1.0, 0.0).astype(jnp.bfloat16)
        for p in range(parts):
            lanes = slice(p * LANES, (p + 1) * LANES)
            table = table_ref[p * count * taps : (p + 1) * count * taps, :]
            mixed = banded(table, keep, source_ref[pl.ds(row, 2 * taps), lanes], taps, count)
            at = (pl.ds(row, taps), lanes)
            q_ref[at] = (mix_ref[at] * mixed).astype(q_ref.dtype)
        return carry

    lax.fori_loop(0, rows // taps, tile, 0)


def backward_kernel(
    taps, count, base_ref, last_ref, head_ref, keys_ref, values_ref, queries_ref, mix_ref,
    k_ref, v_ref, table_ref, source_ref,
):
    rows, width = keys_ref.shape
    parts = width // LANES
    toeplitz_into(table_ref, base_ref, taps, parts * count)
    source_ref[:rows, :] = (mix_ref[...] * queries_ref[...].astype(jnp.float32)).astype(jnp.bfloat16)
    source_ref[rows:, :] = head_ref[...]

    def tile(i, carry):
        row = pl.multiple_of(i * taps, taps)
        at_row = lax.broadcasted_iota(jnp.int32, (taps, 2 * taps), 0) + i * taps
        keep = jnp.where(at_row >= last_ref[:, pl.ds(row, 2 * taps)], 1.0, 0.0).astype(jnp.bfloat16)
        for p in range(parts):
            lanes = slice(p * LANES, (p + 1) * LANES)
            table = table_ref[p * count * taps : (p + 1) * count * taps, :]
            conv = banded(table, keep, source_ref[pl.ds(row, 2 * taps), lanes], taps, count)
            at = (pl.ds(row, taps), lanes)
            k_ref[at] = (conv * values_ref[at].astype(jnp.float32)).astype(k_ref.dtype)
            v_ref[at] = (conv * keys_ref[at].astype(jnp.float32)).astype(v_ref.dtype)
        return carry

    lax.fori_loop(0, rows // taps, tile, 0)


def conv_call(kernel, name, base, last, edge, operands, outs, taps, per, width, start=0):
    rows = operands[0].shape[0]
    cols = min(width, 4 * LANES)
    count = cols // LANES * per
    skip = start // cols
    slab = pl.BlockSpec((rows, cols), lambda g: (0, g + skip))
    return pl.pallas_call(
        functools.partial(kernel, taps, per),
        grid=(width // cols,),
        in_specs=[
            pl.BlockSpec((count, 2 * taps), lambda g: (g + skip, 0)),
            pl.BlockSpec(last.shape, lambda g: (0, 0)),
            pl.BlockSpec((taps, cols), lambda g: (0, g + skip)),
        ]
        + [slab] * len(operands),
        out_specs=[pl.BlockSpec((rows, cols), lambda g: (0, g))] * outs,
        out_shape=[jax.ShapeDtypeStruct((rows, width), jnp.bfloat16)] * outs,
        scratch_shapes=[
            pltpu.VMEM((count * taps, 2 * taps), jnp.bfloat16),
            pltpu.VMEM((rows + taps, cols), jnp.bfloat16),
        ],
        compiler_params=params(1),
        cost_estimate=BRIEF,
        name=name,
    )(base, last, edge, *operands)


NT = (((1,), (1,)), ((), ()))


def mix_kernel(at_ref, *refs):
    lefts, own_ref, sib_ref, out_ref = refs[:-3], *refs[-3:]
    step = pl.program_id(1)
    both = None
    for n, left in enumerate(lefts):
        right = (own_ref, sib_ref)[n % 2][n // 2]
        part = lax.dot_general(left[...], right, NT, preferred_element_type=jnp.float32)
        both = part if both is None else both + part

    @pl.when(step == 0)
    def _():
        out_ref[...] = both

    @pl.when(step > 0)
    def _():
        out_ref[...] += both


def mix_matmul(at, grads, own, sib):
    rows = grads.shape[0]
    blocks, width, feats = own.shape
    cols = min(width, 1024)
    lefts = [
        pl.BlockSpec((rows, feats), lambda n, j, at, side=side, k=k: (0, at[side, 2 * j + k]))
        for k in range(2)
        for side in range(2)
    ]
    right = pl.BlockSpec((2, cols, feats), lambda n, j, at: (j, n, 0))
    return pl.pallas_call(
        mix_kernel,
        grid_spec=pltpu.PrefetchScalarGridSpec(
            num_scalar_prefetch=1,
            grid=(width // cols, blocks // 2),
            in_specs=lefts + [right, right],
            out_specs=pl.BlockSpec((rows, cols), lambda n, j, at: (0, n)),
        ),
        out_shape=jax.ShapeDtypeStruct((rows, width), jnp.float32),
        compiler_params=params(2),
        cost_estimate=BRIEF,
        name="mix_matmul",
    )(at, *[grads] * len(lefts), own, sib)


def project_kernel(places, blocks, *refs):
    half = pl.num_programs(0) // 2
    own, sib = refs[: len(places)], refs[len(places) : 2 * len(places)]
    weights, outs = refs[2 * len(places) : -2], refs[-2:]

    def into(grads, out_ref):
        for n in range(blocks):
            total = None
            for grad, (b, left) in zip(grads, places):
                right = weights[n][b, :, left : left + grad.shape[1]]
                part = lax.dot_general(grad[...], right, NT, preferred_element_type=jnp.float32)
                total = part if total is None else total + part
            out_ref[n] = total.astype(out_ref.dtype)

    @pl.when(pl.program_id(0) < half)
    def _():
        into(own, outs[0])

    @pl.when(pl.program_id(0) >= half)
    def _():
        into(sib, outs[1])


def project(own, sib, weights):
    blocks = len(weights)
    branches, feats, width = weights[0].shape
    rows = own[0][0].shape[0]
    places = [
        (b, sum(p.shape[1] for p in pieces[:at])) for b, pieces in enumerate(own) for at in range(len(pieces))
    ]
    own, sib = [p for pieces in own for p in pieces], [p for pieces in sib for p in pieces]
    half = 2
    step = rows // half

    def first(i):
        return jnp.minimum(i, half - 1)

    def second(i):
        return jnp.maximum(i - half, 0)

    out = jax.ShapeDtypeStruct((blocks, rows, feats), jnp.bfloat16)
    return pl.pallas_call(
        functools.partial(project_kernel, places, blocks),
        grid=(2 * half,),
        in_specs=[pl.BlockSpec((step, p.shape[1]), lambda i: (first(i), 0)) for p in own]
        + [pl.BlockSpec((step, p.shape[1]), lambda i: (second(i), 0)) for p in sib]
        + [
            pl.BlockSpec((branches, feats, width), lambda i: (0, 0, 0), pipeline_mode=pl.Buffered(1))
        ]
        * blocks,
        out_specs=[
            pl.BlockSpec((blocks, step, feats), lambda i: (0, first(i), 0)),
            pl.BlockSpec((blocks, step, feats), lambda i: (0, second(i), 0)),
        ],
        out_shape=[out, out],
        compiler_params=params(1),
        cost_estimate=BRIEF,
        name="project",
    )(*own, *sib, *weights)


def pick_kernel(at_ref, own_ref, sib_ref, input_ref, gain_ref, norm_ref, cross_ref):
    step = pl.program_id(0)
    ours = (lax.broadcasted_iota(jnp.int32, own_ref.shape[1:], 0) * 0 + at_ref[2, step]) == 1
    norm = jnp.where(ours, own_ref[0].astype(jnp.float32), sib_ref[0].astype(jnp.float32))
    norm_ref[...] = norm.astype(norm_ref.dtype)
    part = jnp.sum(
        gain_ref[...].astype(jnp.float32) * norm * input_ref[...].astype(jnp.float32),
        axis=1,
        keepdims=True,
    )

    @pl.when(step == 0)
    def _():
        cross_ref[...] = part

    @pl.when(step > 0)
    def _():
        cross_ref[...] += part


def pick(at, own, sib, block_input, gain):
    rows, width = block_input.shape
    feats = own.shape[2]
    return pl.pallas_call(
        pick_kernel,
        grid_spec=pltpu.PrefetchScalarGridSpec(
            num_scalar_prefetch=1,
            grid=(width // feats,),
            in_specs=[
                pl.BlockSpec((1, rows, feats), lambda j, at: (at[0, j], 0, 0)),
                pl.BlockSpec((1, rows, feats), lambda j, at: (at[1, j], 0, 0)),
                pl.BlockSpec((rows, feats), lambda j, at: (0, j)),
                pl.BlockSpec((1, feats), lambda j, at: (0, j)),
            ],
            out_specs=[
                pl.BlockSpec((rows, feats), lambda j, at: (0, j)),
                pl.BlockSpec((rows, 1), lambda j, at: (0, 0)),
            ],
        ),
        out_shape=[
            jax.ShapeDtypeStruct((rows, width), jnp.bfloat16),
            jax.ShapeDtypeStruct((rows, 1), jnp.float32),
        ],
        compiler_params=params(1),
        cost_estimate=BRIEF,
        name="pick",
    )(at, own, sib, block_input, gain)


def finish_kernel(features, groups, at_ref, *refs):
    input_ref, gain_ref, inverse_ref, grad_ref, out_ref, norm_ref = refs[2 * groups :]
    count, step, feats = norm_ref.shape[1:]
    c = at_ref[2, 0]
    for parity, blocks in ((c, refs[:groups]), (1 - c, refs[groups : 2 * groups])):
        first = 0
        for block in blocks:
            norm_ref[parity, first : first + block.shape[0]] = block[...]
            first += block.shape[0]

    cross = jnp.zeros((step, feats), jnp.float32)
    for n in range(count):
        for parity in range(2):
            block = at_ref[0, n] * 2 + parity
            left = pl.multiple_of(lax.rem(block, count) * feats, feats)
            half = lax.div(block, count)
            gain = gain_ref[half, :, pl.ds(left, feats)].astype(jnp.float32)
            source = input_ref[half, :, pl.ds(left, feats)].astype(jnp.float32)
            cross += gain * norm_ref[parity, n].astype(jnp.float32) * source
    inverse = inverse_ref[...]
    scale = inverse * inverse * inverse * jnp.sum(cross, axis=1, keepdims=True) / features
    for j in range(count):
        cols = slice(j * feats, (j + 1) * feats)
        block = c * count + j
        place = at_ref[1, lax.div(block, 2)]
        scaled = gain_ref[c, :, cols].astype(jnp.float32) * norm_ref[lax.rem(block, 2), place].astype(jnp.float32)
        result = grad_ref[:, cols].astype(jnp.float32) + inverse * scaled
        result -= input_ref[c, :, cols].astype(jnp.float32) * scale
        out_ref[:, cols] = result.astype(out_ref.dtype)


def finish(at, own, sib, inputs, gains, inverse, grad_out):
    rows, width = grad_out.shape
    count, feats = at.shape[1], own[0].shape[2]
    step = min(rows, 128)

    slab = pl.BlockSpec((step, width), lambda i, at: (i, 0))
    return pl.pallas_call(
        functools.partial(finish_kernel, 2 * width, len(own)),
        grid_spec=pltpu.PrefetchScalarGridSpec(
            num_scalar_prefetch=1,
            grid=(rows // step,),
            in_specs=[
                pl.BlockSpec((group.shape[0], step, feats), lambda i, at: (0, i, 0)) for group in (*own, *sib)
            ]
            + [
                pl.BlockSpec((2, step, width), lambda i, at: (0, i, 0)),
                pl.BlockSpec((2, 1, width), lambda i, at: (0, 0, 0)),
                pl.BlockSpec((step, 1), lambda i, at: (i, 0)),
                slab,
            ],
            out_specs=slab,
            scratch_shapes=[pltpu.VMEM((2, count, step, feats), jnp.bfloat16)],
        ),
        out_shape=jax.ShapeDtypeStruct((rows, width), jnp.bfloat16),
        compiler_params=params(1),
        cost_estimate=BRIEF,
        name="finish",
    )(at, *own, *sib, inputs, gains, inverse, grad_out)


def on_device(
    ring,
    n_chan,
    grad_out,
    block_input,
    norm_gain,
    queries,
    keys,
    values,
    filters,
    doc_starts,
    in_weight,
    out_weight,
):
    rows, width = grad_out.shape
    groups, taps = filters.shape
    feats, branches = in_weight.shape[:2]
    count = len(ring)
    per = LANES * groups // width
    features = feats * 2 * count
    o, x, h, c = (lax.axis_index(a) for a in ("o", "x", "h", "c"))
    order = jnp.array(ring, jnp.int32)
    place = jnp.array([ring.index(i) for i in range(count)], jnp.int32)
    position = place[o]
    far = count // 2
    forth = [(ring[i], ring[(i + 1) % count]) for i in range(count)]
    back = [(b, a) for a, b in forth]

    def exchanged(block):
        return lax.ppermute(block, ("x", "c"), SWAP)

    def swapped(block):
        return jnp.where(x == c, block, exchanged(block))

    def sibling(block):
        return lax.ppermute(block, "c", PAIR)

    def both_ways(up, down):
        return lax.ppermute(up, ("o",), forth), lax.ppermute(down, ("o",), back)

    def far_halves(up, down, axis):
        half = up.shape[axis] // 2
        return both_ways(
            lax.slice_in_dim(up, 0, half, axis=axis),
            lax.slice_in_dim(down, half, 2 * half, axis=axis),
        )

    def neighbour(block, distance):
        route = []
        for i in range(count):
            for core in range(2):
                source = i * 2 + core + distance
                if 0 <= source < 2 * count:
                    route += [(source * 2 + side, (i * 2 + side) * 2 + core) for side in range(2)]
        return lax.ppermute(block, ("o", "x", "c"), route)

    starts = swapped(doc_starts)[0]
    prior = neighbour(doc_starts, -1)[0, -1]
    following = neighbour(doc_starts, 1)[0]
    tail = (keys[rows - taps :].astype(jnp.float32) * values[rows - taps :].astype(jnp.float32)).astype(
        jnp.bfloat16
    )
    taps32 = swapped(filters).astype(jnp.float32)
    out_w = swapped(out_weight)
    in_w = jnp.swapaxes(in_weight, 0, 1)
    out_w, in_w, grad_out, taps32, starts, prior, following, tail = fence(
        out_w, in_w, grad_out, taps32, starts, prior, following, tail
    )

    in_recv = exchanged(in_w)
    sib_in, sib_gain = sibling(block_input), sibling(norm_gain)
    blocks = [out_w]
    up = down = out_w
    for s in range(1, far):
        up, down = both_ways(up, down)
        if s == far - 2:
            up, down, in_recv, in_w, grad_out, queries, sib_in, sib_gain = fence(
                up, down, in_recv, in_w, grad_out, queries, sib_in, sib_gain
            )
        blocks += [up, down]
    in_w = jnp.where(x == c, in_w, in_recv)
    half_recv = exchanged(grad_out)
    first_q = exchanged(queries[:taps])
    blocks.append(jnp.concatenate(far_halves(up, down, 0), axis=0))
    own_out = jnp.stack(blocks)
    def in_order(own, sib):
        return jnp.where(c == 0, jnp.stack([own, sib]), jnp.stack([sib, own]))

    inputs, gains = in_order(block_input, sib_in), in_order(norm_gain, sib_gain)[:, None]
    square_sum = jnp.sum(jnp.square(inputs.astype(jnp.float32)), axis=(0, 2))[:, None]
    if n_chan > 1:
        square_sum = lax.psum(square_sum, "h")
    inverse = lax.rsqrt(square_sum / features + EPSILON)
    distances = [0] + [d for s in range(1, far) for d in (-s, s)] + [far]
    sources = order[(position + jnp.array(distances, jnp.int32)) % count]
    wide = width // feats

    def column(parity):
        block = sources * 2 + parity
        owner = block // wide
        side = jnp.where(owner % 2 == x, 0, 1)
        return side * (n_chan * wide) + (owner // 2) * wide + block % wide

    columns = jnp.stack([column(c), column(1 - c)])
    slabs = 2 * count
    backward = [(i + 1, i) for i in range(slabs - 1)]
    positions = jnp.arange(rows, dtype=jnp.int32)

    def last_of(own, before):
        own = jnp.where(own[None, :] <= positions[:, None], own[None, :], -rows)
        return jnp.maximum(jnp.max(own, axis=1), before - rows)

    last_start = last_of(starts, prior)
    padded_last = jnp.concatenate([last_start, last_of(following, starts[-1])[:taps] + rows])[None]
    edge = jnp.zeros((groups, taps), jnp.float32)
    base_back = jnp.concatenate([taps32, edge], axis=1)
    base_fore = jnp.concatenate([edge[:, :1], taps32[:, ::-1], edge[:, 1:]], axis=1)
    (
        own_out, in_w, half_recv, first_q, grad_out, queries, inverse, inputs, gains, padded_last, last_col,
        base_back, base_fore, columns,
    ) = fence(
        own_out, in_w, half_recv, first_q, grad_out, queries, inverse, inputs, gains, padded_last,
        last_start[:, None], base_back, base_fore, columns,
    )

    ahead, behind = {0: in_w}, {0: in_w}
    ahead[1], behind[1] = both_ways(in_w, in_w)
    sib_out = sibling(own_out)
    grad_other = lax.ppermute(grad_out, ("x", "c"), CYCLE)
    grad_other, keys, tail = fence(grad_other, keys, tail)
    k_recv = exchanged(keys)
    tail = neighbour(tail, -1)
    grad_half = jnp.where(x == c, grad_out, half_recv)
    if n_chan > 1:
        grad_half = lax.all_gather(grad_half, "h", axis=1, tiled=True)
        grad_other = lax.all_gather(grad_other, "h", axis=1, tiled=True)
    grads = jnp.concatenate([grad_half, grad_other], axis=1)
    mix_grad = mix_matmul(columns, grads, own_out, sib_out)
    ahead[1], behind[1], mix_grad, k_recv, keys, values = fence(
        ahead[1], behind[1], mix_grad, k_recv, keys, values
    )

    ahead[2], behind[2] = both_ways(ahead[1], behind[1])
    v_recv = exchanged(values)
    head = mix_grad[:taps] * jnp.where(x == c, queries[:taps], first_q).astype(jnp.float32)
    head = lax.ppermute(head.astype(jnp.bfloat16), ("o", "c"), backward)
    own_k = jnp.where(x == c, keys, k_recv)
    v_recv, values, own_k, queries, tail = fence(v_recv, values, own_k, queries, tail)
    q_recv = exchanged(queries)
    own_v = jnp.where(x == c, values, v_recv)
    middle = width // 2

    def halves(kernel, name, *operands, outs):
        return [
            conv_call(kernel, name, *operands, outs, taps, per, middle, start) for start in (0, middle)
        ]

    (q_left,), (q_right,) = halves(
        forward_kernel, "forward_conv", base_fore, last_col, tail, [own_k, own_v, mix_grad], outs=1
    )
    sib_left = sibling(q_left)
    ahead[2], behind[2], q_left, q_right, sib_left, head, q_recv, queries = fence(
        ahead[2], behind[2], q_left, q_right, sib_left, head, q_recv, queries
    )

    upper, lower = slice(0, feats // 2), slice(feats // 2, feats)
    early = both_ways(ahead[2][:, upper], behind[2][:, upper])
    late = both_ways(ahead[2][:, lower], behind[2][:, lower])
    own_q = jnp.where(x == c, queries, q_recv)
    grads = []
    for start in (0, middle):
        k_half, v_half = conv_call(
            backward_kernel, "backward_conv", base_back, padded_last, head, [own_k, own_v, own_q, mix_grad], 2,
            taps, per, middle, start,
        )
        if start > 0:
            *early, k_half, v_half = fence(*early, k_half, v_half)
        grads.append((k_half, v_half))
    own_grads = [[q_left, q_right]] + [[half[b] for half in grads] for b in range(2)]
    sib_grads = [[sib_left, sibling(q_right)]] + [[sibling(half[b]) for half in grads] for b in range(2)]

    def partial_sums(weights):
        ours, theirs = project(own_grads, sib_grads, weights)
        return jnp.where(c == x, ours, theirs), jnp.where(c == x, theirs, ours)

    def summed(keep, received):
        return (keep.astype(jnp.float32) + received.astype(jnp.float32)).astype(jnp.bfloat16)

    def over_x(block):
        return lax.ppermute(block, "x", PAIR)

    keep, send = partial_sums([in_w, ahead[1], behind[1]])
    *early, late_up, late_down, keep, send = fence(*early, *late, keep, send)
    ahead[3] = jnp.concatenate([early[0], late_up], axis=1)
    behind[3] = jnp.concatenate([early[1], late_down], axis=1)
    norms = []
    for s in range(4, far + 1):
        if s < far:
            up, down = both_ways(ahead[s - 1], behind[s - 1])
        else:
            up, down = far_halves(ahead[s - 1], behind[s - 1], 1)
        arrived = [(keep, over_x(send))]
        if s == 4:
            keep, send = partial_sums([ahead[2], behind[2]])
            keep, send, last_tail = fence(keep, send, own_grads[2][1])
            own_grads[2][1] = last_tail
            arrived.append((keep, over_x(send)))
        keep, send = partial_sums([ahead[s - 1], behind[s - 1]])
        flat = [block for pair in arrived for block in pair]
        up, down, keep, send, *flat = fence(up, down, keep, send, *flat)
        norms += [summed(*flat[i : i + 2]) for i in range(0, len(flat), 2)]
        ahead[s], behind[s] = up, down
    far_keep, far_send = partial_sums([jnp.concatenate([up, down], axis=1)])
    norms += [summed(keep, over_x(send)), summed(far_keep, over_x(far_send))]
    slot = jnp.zeros((count,), jnp.int32).at[sources].set(jnp.arange(count, dtype=jnp.int32))
    if n_chan == 1:
        others = [sibling(n) for n in norms]
        at = jnp.stack([sources, slot, jnp.full((count,), c, jnp.int32)])
        return finish(at, norms, others, inputs, gains, inverse, grad_out)

    norm = lax.psum_scatter(
        jnp.take(jnp.concatenate(norms, axis=0), slot, axis=0), "h", scatter_dimension=0, tiled=True
    )
    other = sibling(norm)
    mine = (h * 2 + c) * wide + jnp.arange(wide, dtype=jnp.int32)
    slots = mine // 2 - h * (count // n_chan)
    at = jnp.stack([slots, slots, (mine % 2 == c).astype(jnp.int32)])
    norm_grad, cross = pick(at, norm, other, block_input, norm_gain[None])
    cross_sum = lax.psum(cross, ("h", "c"))
    scaled = norm_gain.astype(jnp.float32)[None, :] * norm_grad.astype(jnp.float32)
    result = (
        grad_out.astype(jnp.float32)
        + inverse * scaled
        - block_input.astype(jnp.float32) * (inverse * inverse * inverse) * cross_sum / features
    )
    return result.astype(jnp.bfloat16)


def solution(mesh):
    outer, n_chan = mesh.shape["ctx"] // 2, mesh.shape["ch"] // 2
    split = Mesh(mesh.devices.reshape(outer, 2, n_chan, 2), ("o", "x", "h", "c"))
    ring = list(range(0, outer, 2)) + list(range(outer - 1, 0, -2))
    tok, chan = ("o", "x"), ("h", "c")
    placed = (
        P(tok, chan),
        P(tok, chan),
        P(chan),
        P(tok, chan),
        P(tok, chan),
        P(tok, chan),
        P(chan, None),
        P(tok, None),
        P(tok, None, chan),
        P(chan, tok),
    )
    return jax.shard_map(
        functools.partial(on_device, ring, n_chan),
        mesh=split,
        in_specs=placed,
        out_specs=P(tok, chan),
        check_vma=False,
    )
```

```python
import functools

import jax
import jax.numpy as jnp
from jax import lax
from jax.experimental import pallas as pl
from jax.experimental.pallas import tpu as pltpu
from jax.sharding import Mesh
from jax.sharding import PartitionSpec as P

LANES = 128
EPSILON = 1e-05
VMEM_BYTES = 52 * 1024 * 1024

BRIEF = pl.CostEstimate(flops=1024, bytes_accessed=1024, transcendentals=0)

SWAP = [(1, 2), (2, 1)]
CYCLE = [(0, 2), (1, 0), (2, 3), (3, 1)]
PAIR = [(0, 1), (1, 0)]


def fence(*blocks):
    return lax.optimization_barrier(blocks)


def params(parallel):
    return pltpu.CompilerParams(
        dimension_semantics=("arbitrary",) * parallel, vmem_limit_bytes=VMEM_BYTES
    )


def toeplitz_into(table_ref, base_ref, taps, count):
    for q in range(count):
        row = jnp.broadcast_to(base_ref[q : q + 1, :], (taps, 2 * taps))
        band = pltpu.roll(row, 0, 1, stride=1, stride_axis=0)
        table_ref[q * taps : (q + 1) * taps, :] = band.astype(table_ref.dtype)


def banded(table, keep, source, taps, count):
    table = table.reshape(count, taps, 2 * taps)
    masked = (table * keep[None]).reshape(count * taps, 2 * taps)
    wide = jnp.dot(masked, source, preferred_element_type=jnp.float32)
    width = source.shape[1]
    owner = lax.broadcasted_iota(jnp.int32, (taps, width), 1) // (width // count)
    total = wide[:taps]
    for q in range(1, count):
        total = jnp.where(owner == q, wide[q * taps : (q + 1) * taps], total)
    return total


def forward_kernel(
    taps, count, own_ref, base_ref, last_ref, tail_ref, keys_ref, mix_ref, values_ref, other_values_ref,
    q_ref, table_ref, source_ref,
):
    rows, width = keys_ref.shape
    parts = width // LANES
    toeplitz_into(table_ref, base_ref, taps, parts * count)
    source_ref[:taps, :] = tail_ref[...]
    for flag, ref in ((1, values_ref), (0, other_values_ref)):

        @pl.when(own_ref[0, 0] == flag)
        def _(ref=ref):
            source_ref[taps:, :] = (keys_ref[...].astype(jnp.float32) * ref[...].astype(jnp.float32)).astype(
                jnp.bfloat16
            )

    def tile(i, carry):
        row = pl.multiple_of(i * taps, taps)
        col = lax.broadcasted_iota(jnp.int32, (taps, 2 * taps), 1) + (i - 1) * taps
        keep = jnp.where(col >= last_ref[pl.ds(row, taps), :], 1.0, 0.0).astype(jnp.bfloat16)
        for p in range(parts):
            lanes = slice(p * LANES, (p + 1) * LANES)
            table = table_ref[p * count * taps : (p + 1) * count * taps, :]
            mixed = banded(table, keep, source_ref[pl.ds(row, 2 * taps), lanes], taps, count)
            at = (pl.ds(row, taps), lanes)
            q_ref[at] = (mix_ref[at] * mixed).astype(q_ref.dtype)
        return carry

    lax.fori_loop(0, rows // taps, tile, 0)


def backward_kernel(
    taps, count, own_ref, base_ref, last_ref, head_ref, keys_ref, mix_ref, values_ref, other_values_ref,
    queries_ref, other_queries_ref, k_ref, v_ref, table_ref, source_ref, held_ref,
):
    rows, width = keys_ref.shape
    parts = width // LANES
    toeplitz_into(table_ref, base_ref, taps, parts * count)
    source_ref[rows:, :] = head_ref[...]
    for flag, values, queries in ((1, values_ref, queries_ref), (0, other_values_ref, other_queries_ref)):

        @pl.when(own_ref[0, 0] == flag)
        def _(values=values, queries=queries):
            source_ref[:rows, :] = (mix_ref[...] * queries[...].astype(jnp.float32)).astype(jnp.bfloat16)
            held_ref[...] = values[...]

    def tile(i, carry):
        row = pl.multiple_of(i * taps, taps)
        at_row = lax.broadcasted_iota(jnp.int32, (taps, 2 * taps), 0) + i * taps
        keep = jnp.where(at_row >= last_ref[:, pl.ds(row, 2 * taps)], 1.0, 0.0).astype(jnp.bfloat16)
        for p in range(parts):
            lanes = slice(p * LANES, (p + 1) * LANES)
            table = table_ref[p * count * taps : (p + 1) * count * taps, :]
            conv = banded(table, keep, source_ref[pl.ds(row, 2 * taps), lanes], taps, count)
            at = (pl.ds(row, taps), lanes)
            k_ref[at] = (conv * held_ref[at].astype(jnp.float32)).astype(k_ref.dtype)
            v_ref[at] = (conv * keys_ref[at].astype(jnp.float32)).astype(v_ref.dtype)
        return carry

    lax.fori_loop(0, rows // taps, tile, 0)


def conv_call(kernel, name, own, base, last, edge, operands, outs, taps, per, width, start=0):
    rows = operands[0].shape[0]
    cols = min(width, 4 * LANES)
    count = cols // LANES * per
    skip = start // cols
    slab = pl.BlockSpec((rows, cols), lambda g: (0, g + skip))
    return pl.pallas_call(
        functools.partial(kernel, taps, per),
        grid=(width // cols,),
        in_specs=[
            pl.BlockSpec(memory_space=pltpu.SMEM),
            pl.BlockSpec((count, 2 * taps), lambda g: (g + skip, 0)),
            pl.BlockSpec(last.shape, lambda g: (0, 0)),
            pl.BlockSpec((taps, cols), lambda g: (0, g + skip)),
        ]
        + [slab] * len(operands),
        out_specs=[pl.BlockSpec((rows, cols), lambda g: (0, g))] * outs,
        out_shape=[jax.ShapeDtypeStruct((rows, width), jnp.bfloat16)] * outs,
        scratch_shapes=[
            pltpu.VMEM((count * taps, 2 * taps), jnp.bfloat16),
            pltpu.VMEM((rows + taps, cols), jnp.bfloat16),
        ]
        + [pltpu.VMEM((rows, cols), jnp.bfloat16)] * (outs - 1),
        compiler_params=params(1),
        cost_estimate=BRIEF,
        name=name,
    )(own, base, last, edge, *operands)


NT = (((1,), (1,)), ((), ()))


def mix_kernel(at_ref, *refs):
    lefts, own_ref, sib_ref, out_ref = refs[:-3], *refs[-3:]
    step = pl.program_id(1)
    both = None
    for n, left in enumerate(lefts):
        right = (own_ref, sib_ref)[n % 2][n // 2]
        part = lax.dot_general(left[...], right, NT, preferred_element_type=jnp.float32)
        both = part if both is None else both + part

    @pl.when(step == 0)
    def _():
        out_ref[...] = both

    @pl.when(step > 0)
    def _():
        out_ref[...] += both


def mix_matmul(at, grads, own, sib):
    rows = grads.shape[0]
    blocks, width, feats = own.shape
    cols = min(width, 1024)
    lefts = [
        pl.BlockSpec((rows, feats), lambda n, j, at, side=side, k=k: (0, at[side, 2 * j + k]))
        for k in range(2)
        for side in range(2)
    ]
    right = pl.BlockSpec((2, cols, feats), lambda n, j, at: (j, n, 0))
    return pl.pallas_call(
        mix_kernel,
        grid_spec=pltpu.PrefetchScalarGridSpec(
            num_scalar_prefetch=1,
            grid=(width // cols, blocks // 2),
            in_specs=lefts + [right, right],
            out_specs=pl.BlockSpec((rows, cols), lambda n, j, at: (0, n)),
        ),
        out_shape=jax.ShapeDtypeStruct((rows, width), jnp.float32),
        compiler_params=params(2),
        cost_estimate=BRIEF,
        name="mix_matmul",
    )(at, *[grads] * len(lefts), own, sib)


def project_kernel(places, pieces, *refs):
    half = pl.num_programs(0) // 2
    own, sib = refs[: len(places)], refs[len(places) : 2 * len(places)]
    parts, refs = refs[2 * len(places) : 2 * len(places) + sum(pieces)], refs[2 * len(places) + sum(pieces) :]
    outs, joined = refs[:2], list(refs[2:])
    blocks, weights, first = len(pieces), [], 0
    for number in pieces:
        block = parts[first : first + number]
        first += number
        if number == 1:
            weights.append(block[0])
            continue
        whole = joined.pop(0)
        weights.append(whole)

        @pl.when(pl.program_id(0) == 0)
        def _(block=block, whole=whole):
            top = 0
            for part in block:
                whole[:, top : top + part.shape[1], :] = part[...]
                top += part.shape[1]

    def into(grads, out_ref):
        for n in range(blocks):
            total = None
            for grad, (b, left) in zip(grads, places):
                right = weights[n][b, :, left : left + grad.shape[1]]
                part = lax.dot_general(grad[...], right, NT, preferred_element_type=jnp.float32)
                total = part if total is None else total + part
            out_ref[n] = total.astype(out_ref.dtype)

    @pl.when(pl.program_id(0) < half)
    def _():
        into(own, outs[0])

    @pl.when(pl.program_id(0) >= half)
    def _():
        into(sib, outs[1])


def project(own, sib, weights):
    weights = [w if isinstance(w, tuple) else (w,) for w in weights]
    blocks, pieces = len(weights), [len(w) for w in weights]
    branches, _, width = weights[0][0].shape
    feats = sum(part.shape[1] for part in weights[0])
    rows = own[0][0].shape[0]
    places = [
        (b, sum(p.shape[1] for p in pieces[:at])) for b, pieces in enumerate(own) for at in range(len(pieces))
    ]
    own, sib = [p for pieces in own for p in pieces], [p for pieces in sib for p in pieces]
    half = 2
    step = rows // half

    def first(i):
        return jnp.minimum(i, half - 1)

    def second(i):
        return jnp.maximum(i - half, 0)

    out = jax.ShapeDtypeStruct((blocks, rows, feats), jnp.bfloat16)
    return pl.pallas_call(
        functools.partial(project_kernel, places, pieces),
        grid=(2 * half,),
        in_specs=[pl.BlockSpec((step, p.shape[1]), lambda i: (first(i), 0)) for p in own]
        + [pl.BlockSpec((step, p.shape[1]), lambda i: (second(i), 0)) for p in sib]
        + [
            pl.BlockSpec(part.shape, lambda i: (0, 0, 0), pipeline_mode=pl.Buffered(1))
            for block in weights
            for part in block
        ],
        out_specs=[
            pl.BlockSpec((blocks, step, feats), lambda i: (0, first(i), 0)),
            pl.BlockSpec((blocks, step, feats), lambda i: (0, second(i), 0)),
        ],
        out_shape=[out, out],
        scratch_shapes=[pltpu.VMEM((branches, feats, width), jnp.bfloat16)] * sum(n > 1 for n in pieces),
        compiler_params=params(1),
        cost_estimate=BRIEF,
        name="project",
    )(*own, *sib, *[part for block in weights for part in block])


def pick_kernel(at_ref, own_ref, sib_ref, input_ref, gain_ref, norm_ref, cross_ref):
    step = pl.program_id(0)
    ours = (lax.broadcasted_iota(jnp.int32, own_ref.shape[1:], 0) * 0 + at_ref[2, step]) == 1
    norm = jnp.where(ours, own_ref[0].astype(jnp.float32), sib_ref[0].astype(jnp.float32))
    norm_ref[...] = norm.astype(norm_ref.dtype)
    part = jnp.sum(
        gain_ref[...].astype(jnp.float32) * norm * input_ref[...].astype(jnp.float32),
        axis=1,
        keepdims=True,
    )

    @pl.when(step == 0)
    def _():
        cross_ref[...] = part

    @pl.when(step > 0)
    def _():
        cross_ref[...] += part


def pick(at, own, sib, block_input, gain):
    rows, width = block_input.shape
    feats = own.shape[2]
    return pl.pallas_call(
        pick_kernel,
        grid_spec=pltpu.PrefetchScalarGridSpec(
            num_scalar_prefetch=1,
            grid=(width // feats,),
            in_specs=[
                pl.BlockSpec((1, rows, feats), lambda j, at: (at[0, j], 0, 0)),
                pl.BlockSpec((1, rows, feats), lambda j, at: (at[1, j], 0, 0)),
                pl.BlockSpec((rows, feats), lambda j, at: (0, j)),
                pl.BlockSpec((1, feats), lambda j, at: (0, j)),
            ],
            out_specs=[
                pl.BlockSpec((rows, feats), lambda j, at: (0, j)),
                pl.BlockSpec((rows, 1), lambda j, at: (0, 0)),
            ],
        ),
        out_shape=[
            jax.ShapeDtypeStruct((rows, width), jnp.bfloat16),
            jax.ShapeDtypeStruct((rows, 1), jnp.float32),
        ],
        compiler_params=params(1),
        cost_estimate=BRIEF,
        name="pick",
    )(at, own, sib, block_input, gain)


def finish_kernel(features, groups, at_ref, *refs):
    input_ref, gain_ref, inverse_ref, grad_ref, out_ref, norm_ref = refs[2 * groups :]
    count, step, feats = norm_ref.shape[1:]
    c = at_ref[2, 0]
    for parity, blocks in ((c, refs[:groups]), (1 - c, refs[groups : 2 * groups])):
        first = 0
        for block in blocks:
            norm_ref[parity, first : first + block.shape[0]] = block[...]
            first += block.shape[0]

    cross = jnp.zeros((step, feats), jnp.float32)
    for n in range(count):
        for parity in range(2):
            block = at_ref[0, n] * 2 + parity
            left = pl.multiple_of(lax.rem(block, count) * feats, feats)
            half = lax.div(block, count)
            gain = gain_ref[half, :, pl.ds(left, feats)].astype(jnp.float32)
            source = input_ref[half, :, pl.ds(left, feats)].astype(jnp.float32)
            cross += gain * norm_ref[parity, n].astype(jnp.float32) * source
    inverse = inverse_ref[...]
    scale = inverse * inverse * inverse * jnp.sum(cross, axis=1, keepdims=True) / features
    for j in range(count):
        cols = slice(j * feats, (j + 1) * feats)
        block = c * count + j
        place = at_ref[1, lax.div(block, 2)]
        scaled = gain_ref[c, :, cols].astype(jnp.float32) * norm_ref[lax.rem(block, 2), place].astype(jnp.float32)
        result = grad_ref[:, cols].astype(jnp.float32) + inverse * scaled
        result -= input_ref[c, :, cols].astype(jnp.float32) * scale
        out_ref[:, cols] = result.astype(out_ref.dtype)


def finish(at, own, sib, inputs, gains, inverse, grad_out):
    rows, width = grad_out.shape
    count, feats = at.shape[1], own[0].shape[2]
    step = min(rows, 128)

    slab = pl.BlockSpec((step, width), lambda i, at: (i, 0))
    return pl.pallas_call(
        functools.partial(finish_kernel, 2 * width, len(own)),
        grid_spec=pltpu.PrefetchScalarGridSpec(
            num_scalar_prefetch=1,
            grid=(rows // step,),
            in_specs=[
                pl.BlockSpec((group.shape[0], step, feats), lambda i, at: (0, i, 0)) for group in (*own, *sib)
            ]
            + [
                pl.BlockSpec((2, step, width), lambda i, at: (0, i, 0)),
                pl.BlockSpec((2, 1, width), lambda i, at: (0, 0, 0)),
                pl.BlockSpec((step, 1), lambda i, at: (i, 0)),
                slab,
            ],
            out_specs=slab,
            scratch_shapes=[pltpu.VMEM((2, count, step, feats), jnp.bfloat16)],
        ),
        out_shape=jax.ShapeDtypeStruct((rows, width), jnp.bfloat16),
        compiler_params=params(1),
        cost_estimate=BRIEF,
        name="finish",
    )(at, *own, *sib, inputs, gains, inverse, grad_out)


def on_device(
    ring,
    n_chan,
    grad_out,
    block_input,
    norm_gain,
    queries,
    keys,
    values,
    filters,
    doc_starts,
    in_weight,
    out_weight,
):
    rows, width = grad_out.shape
    groups, taps = filters.shape
    feats, branches = in_weight.shape[:2]
    count = len(ring)
    per = LANES * groups // width
    features = feats * 2 * count
    o, x, h, c = (lax.axis_index(a) for a in ("o", "x", "h", "c"))
    order = jnp.array(ring, jnp.int32)
    place = jnp.array([ring.index(i) for i in range(count)], jnp.int32)
    position = place[o]
    far = count // 2
    forth = [(ring[i], ring[(i + 1) % count]) for i in range(count)]
    back = [(b, a) for a, b in forth]

    def exchanged(block):
        return lax.ppermute(block, ("x", "c"), SWAP)

    def swapped(block):
        return jnp.where(x == c, block, exchanged(block))

    def sibling(block):
        return lax.ppermute(block, "c", PAIR)

    def both_ways(up, down):
        return lax.ppermute(up, ("o",), forth), lax.ppermute(down, ("o",), back)

    def far_halves(up, down, axis):
        half = up.shape[axis] // 2
        return both_ways(
            lax.slice_in_dim(up, 0, half, axis=axis),
            lax.slice_in_dim(down, half, 2 * half, axis=axis),
        )

    def neighbour(block, distance):
        route = []
        for i in range(count):
            for core in range(2):
                source = i * 2 + core + distance
                if 0 <= source < 2 * count:
                    route += [(source * 2 + side, (i * 2 + side) * 2 + core) for side in range(2)]
        return lax.ppermute(block, ("o", "x", "c"), route)

    starts = swapped(doc_starts)[0]
    prior = neighbour(doc_starts, -1)[0, -1]
    following = neighbour(doc_starts, 1)[0]
    tail = (keys[rows - taps :].astype(jnp.float32) * values[rows - taps :].astype(jnp.float32)).astype(
        jnp.bfloat16
    )
    taps32 = swapped(filters).astype(jnp.float32)
    out_w = swapped(out_weight)
    in_w = jnp.swapaxes(in_weight, 0, 1)
    out_w, in_w, grad_out, taps32, starts, prior, following, tail = fence(
        out_w, in_w, grad_out, taps32, starts, prior, following, tail
    )

    in_recv = exchanged(in_w)
    sib_in, sib_gain = sibling(block_input), sibling(norm_gain)
    blocks = [out_w]
    up = down = out_w
    for s in range(1, far):
        up, down = both_ways(up, down)
        if s == far - 2:
            up, down, in_recv, in_w, grad_out, queries, sib_in, sib_gain = fence(
                up, down, in_recv, in_w, grad_out, queries, sib_in, sib_gain
            )
        blocks += [up, down]
    in_w = jnp.where(x == c, in_w, in_recv)
    half_recv = exchanged(grad_out)
    first_q = exchanged(queries[:taps])
    blocks.append(jnp.concatenate(far_halves(up, down, 0), axis=0))
    own_out = jnp.stack(blocks)
    def in_order(own, sib):
        return jnp.where(c == 0, jnp.stack([own, sib]), jnp.stack([sib, own]))

    inputs, gains = in_order(block_input, sib_in), in_order(norm_gain, sib_gain)[:, None]
    square_sum = jnp.sum(jnp.square(inputs.astype(jnp.float32)), axis=(0, 2))[:, None]
    if n_chan > 1:
        square_sum = lax.psum(square_sum, "h")
    inverse = lax.rsqrt(square_sum / features + EPSILON)
    distances = [0] + [d for s in range(1, far) for d in (-s, s)] + [far]
    sources = order[(position + jnp.array(distances, jnp.int32)) % count]
    wide = width // feats

    def column(parity):
        block = sources * 2 + parity
        owner = block // wide
        side = jnp.where(owner % 2 == x, 0, 1)
        return side * (n_chan * wide) + (owner // 2) * wide + block % wide

    columns = jnp.stack([column(c), column(1 - c)])
    slabs = 2 * count
    backward = [(i + 1, i) for i in range(slabs - 1)]
    positions = jnp.arange(rows, dtype=jnp.int32)

    def last_of(own, before):
        own = jnp.where(own[None, :] <= positions[:, None], own[None, :], -rows)
        return jnp.maximum(jnp.max(own, axis=1), before - rows)

    last_start = last_of(starts, prior)
    padded_last = jnp.concatenate([last_start, last_of(following, starts[-1])[:taps] + rows])[None]
    edge = jnp.zeros((groups, taps), jnp.float32)
    base_back = jnp.concatenate([taps32, edge], axis=1)
    base_fore = jnp.concatenate([edge[:, :1], taps32[:, ::-1], edge[:, 1:]], axis=1)
    (
        own_out, in_w, half_recv, first_q, grad_out, queries, inverse, inputs, gains, padded_last, last_col,
        base_back, base_fore, columns,
    ) = fence(
        own_out, in_w, half_recv, first_q, grad_out, queries, inverse, inputs, gains, padded_last,
        last_start[:, None], base_back, base_fore, columns,
    )

    ahead, behind = {0: in_w}, {0: in_w}
    ahead[1], behind[1] = both_ways(in_w, in_w)
    sib_out = sibling(own_out)
    grad_other = lax.ppermute(grad_out, ("x", "c"), CYCLE)
    grad_other, keys, tail = fence(grad_other, keys, tail)
    k_recv = exchanged(keys)
    tail = neighbour(tail, -1)
    grad_half = jnp.where(x == c, grad_out, half_recv)
    if n_chan > 1:
        grad_half = lax.all_gather(grad_half, "h", axis=1, tiled=True)
        grad_other = lax.all_gather(grad_other, "h", axis=1, tiled=True)
    grads = jnp.concatenate([grad_half, grad_other], axis=1)
    mix_grad = mix_matmul(columns, grads, own_out, sib_out)
    ahead[1], behind[1], mix_grad, k_recv, keys, values = fence(
        ahead[1], behind[1], mix_grad, k_recv, keys, values
    )

    ahead[2], behind[2] = both_ways(ahead[1], behind[1])
    v_recv = exchanged(values)
    head = mix_grad[:taps] * jnp.where(x == c, queries[:taps], first_q).astype(jnp.float32)
    head = lax.ppermute(head.astype(jnp.bfloat16), ("o", "c"), backward)
    own_k = jnp.where(x == c, keys, k_recv)
    v_recv, values, own_k, queries, tail = fence(v_recv, values, own_k, queries, tail)
    q_recv = exchanged(queries)
    ours = (x == c).astype(jnp.int32).reshape(1, 1)
    middle = width // 2

    def halves(kernel, name, *operands, outs):
        return [
            conv_call(kernel, name, *operands, outs, taps, per, middle, start) for start in (0, middle)
        ]

    (q_left,), (q_right,) = halves(
        forward_kernel, "forward_conv", ours, base_fore, last_col, tail, [own_k, mix_grad, values, v_recv], outs=1
    )
    sib_left = sibling(q_left)
    ahead[2], behind[2], q_left, q_right, sib_left, head, q_recv, queries = fence(
        ahead[2], behind[2], q_left, q_right, sib_left, head, q_recv, queries
    )

    upper, lower = slice(0, feats // 2), slice(feats // 2, feats)
    early = both_ways(ahead[2][:, upper], behind[2][:, upper])
    late = both_ways(ahead[2][:, lower], behind[2][:, lower])
    grads = []
    for start in (0, middle):
        k_half, v_half = conv_call(
            backward_kernel, "backward_conv", ours, base_back, padded_last, head,
            [own_k, mix_grad, values, v_recv, queries, q_recv], 2, taps, per, middle, start,
        )
        if start > 0:
            *early, k_half, v_half = fence(*early, k_half, v_half)
        grads.append((k_half, v_half))
    own_grads = [[q_left, q_right]] + [[half[b] for half in grads] for b in range(2)]
    sib_grads = [[sib_left, sibling(q_right)]] + [[sibling(half[b]) for half in grads] for b in range(2)]

    def partial_sums(weights):
        ours, theirs = project(own_grads, sib_grads, weights)
        return jnp.where(c == x, ours, theirs), jnp.where(c == x, theirs, ours)

    def summed(keep, received):
        return (keep.astype(jnp.float32) + received.astype(jnp.float32)).astype(jnp.bfloat16)

    def over_x(block):
        return lax.ppermute(block, "x", PAIR)

    keep, send = partial_sums([in_w, ahead[1], behind[1]])
    *early, late_up, late_down, keep, send = fence(*early, *late, keep, send)
    ahead[3] = jnp.concatenate([early[0], late_up], axis=1)
    behind[3] = jnp.concatenate([early[1], late_down], axis=1)
    norms = []
    for s in range(4, far + 1):
        if s < far:
            up, down = both_ways(ahead[s - 1], behind[s - 1])
        else:
            up, down = far_halves(ahead[s - 1], behind[s - 1], 1)
        arrived = [(keep, over_x(send))]
        if s == 4:
            keep, send = partial_sums([ahead[2], behind[2]])
            keep, send, last_tail = fence(keep, send, own_grads[2][1])
            own_grads[2][1] = last_tail
            arrived.append((keep, over_x(send)))
        keep, send = partial_sums(
            [(early[0], late_up), (early[1], late_down)] if s == 4 else [ahead[s - 1], behind[s - 1]]
        )
        flat = [block for pair in arrived for block in pair]
        up, down, keep, send, *flat = fence(up, down, keep, send, *flat)
        norms += [summed(*flat[i : i + 2]) for i in range(0, len(flat), 2)]
        ahead[s], behind[s] = up, down
    far_keep, far_send = partial_sums([(up, down)])
    norms += [summed(keep, over_x(send)), summed(far_keep, over_x(far_send))]
    slot = jnp.zeros((count,), jnp.int32).at[sources].set(jnp.arange(count, dtype=jnp.int32))
    if n_chan == 1:
        others = [sibling(n) for n in norms]
        at = jnp.stack([sources, slot, jnp.full((count,), c, jnp.int32)])
        return finish(at, norms, others, inputs, gains, inverse, grad_out)

    norm = lax.psum_scatter(
        jnp.take(jnp.concatenate(norms, axis=0), slot, axis=0), "h", scatter_dimension=0, tiled=True
    )
    other = sibling(norm)
    mine = (h * 2 + c) * wide + jnp.arange(wide, dtype=jnp.int32)
    slots = mine // 2 - h * (count // n_chan)
    at = jnp.stack([slots, slots, (mine % 2 == c).astype(jnp.int32)])
    norm_grad, cross = pick(at, norm, other, block_input, norm_gain[None])
    cross_sum = lax.psum(cross, ("h", "c"))
    scaled = norm_gain.astype(jnp.float32)[None, :] * norm_grad.astype(jnp.float32)
    result = (
        grad_out.astype(jnp.float32)
        + inverse * scaled
        - block_input.astype(jnp.float32) * (inverse * inverse * inverse) * cross_sum / features
    )
    return result.astype(jnp.bfloat16)


def solution(mesh):
    outer, n_chan = mesh.shape["ctx"] // 2, mesh.shape["ch"] // 2
    split = Mesh(mesh.devices.reshape(outer, 2, n_chan, 2), ("o", "x", "h", "c"))
    ring = list(range(0, outer, 2)) + list(range(outer - 1, 0, -2))
    tok, chan = ("o", "x"), ("h", "c")
    placed = (
        P(tok, chan),
        P(tok, chan),
        P(chan),
        P(tok, chan),
        P(tok, chan),
        P(tok, chan),
        P(chan, None),
        P(tok, None),
        P(tok, None, chan),
        P(chan, tok),
    )
    return jax.shard_map(
        functools.partial(on_device, ring, n_chan),
        mesh=split,
        in_specs=placed,
        out_specs=P(tok, chan),
        check_vma=False,
    )
```
